512 devices in a mesh: leaf: 64 (over x, z, core), site: 8 (over y).
Axes of the slice: x: 4, y: 8, z: 8, core: 2. Of those that a mesh axis runs over, the one named last changes fastest.
Arguments:
- tips: float32 [512, 64, 1024], P('leaf', None, 'site'), as said below
- parents: int32 [896], P('leaf'), may hold values from 8 to 14, as said below
- branch_lengths: float32 [896], P('leaf'), may hold values from 0.02 to 0.6
- top_parents: int32 [126], replicated, may hold values from 64 to 126, as said below
- top_lengths: float32 [126], replicated, may hold values from 0.02 to 0.6
- weights: int32 [1024], P('site'), may hold values from 1 to 16
- eig_vectors: float32 [64, 64], replicated, as said below
- eig_inverse: float32 [64, 64], replicated, as said below
- eig_values: float32 [64], replicated, as said below
- labeled_rates: float32 [64, 64], replicated, as said below
- root_freq: float32 [64], replicated, as said below
Outputs:
- local_counts: float32 [896], P('leaf')
- top_counts: float32 [126], replicated
- site_loglik: float32 [1024], P('site')
The draws below stay inside these ranges and needn't reach their ends.
Inputs may be any that keep to these rules, and one draw needn't show every extreme that they name: `parents`: within each block of 14 entries (one subtree) the entries form a binary tree: every entry is larger than its own position in the block, every internal node 8 to 14 is named by exactly two entries. `top_parents`: A binary tree over the subtrees: every entry is larger than its own position, every node 64 to 2 * 64 - 2 is named by exactly two entries. `tips`: Positive. eig_vectors diag(eig_values) eig_inverse is a reversible rate matrix Q on the first 61 states with stationary frequencies root_freq and mean rate 1, and eig_inverse eig_vectors is the identity; rows, columns and eigenvalues past 61 are those of the identity and 0. `eig_inverse`: the inverse of eig_vectors, as above. `eig_values`: eigenvalues of Q, at most 0. `labeled_rates`: Off-diagonal rates of Q for a symmetric set of counted state pairs, 0 elsewhere. `root_freq`: positive on the first 61 states, 0 past them, summing to 1.
All inputs are finite; a program needn't handle non-finite values.
Results may differ from the reference program's by a relative error of at most 0.0003.
Values sent between devices are 32-bit elements; how exact they have to be, the bound alone decides.
A program may use at most 64 MiB of HBM per device.

```python
import math
import jax
import jax.numpy as jnp
from jax import lax

STATES = 64
CODONS = 61
LEAVES_DEV = 8
TAXA = 512
SITES = 1024
BR_DEV = 14
BRANCHES = 896
TOP_BR = 126
N_LEAF = 64


def random_tree(seed_key, leaf_count):
    active = jnp.arange(leaf_count, dtype=jnp.int32)
    parent = jnp.zeros((2 * leaf_count - 2,), jnp.int32)

    def merge_step(counter, state_triple):
        active, parent, seed_key = state_triple
        seed_key, first_key, second_key = jax.random.split(seed_key, 3)
        remaining = leaf_count - counter
        first = jax.random.randint(first_key, (), 0, remaining)
        second = jax.random.randint(second_key, (), 0, remaining - 1)
        second = second + (second >= first).astype(jnp.int32)
        newest = (leaf_count + counter).astype(jnp.int32)
        parent = parent.at[active[first]].set(newest).at[active[second]].set(newest)
        lowest = jnp.minimum(first, second)
        highest = jnp.maximum(first, second)
        last_node = active[remaining - 1]
        active = active.at[lowest].set(newest)
        active = active.at[highest].set(last_node)
        return (active, parent, seed_key)
    _, parent, _ = lax.fori_loop(0, leaf_count - 1, merge_step, (active, parent, seed_key))
    return parent


def draw_parents(key, part):
    groups = BRANCHES // BR_DEV
    indices = jnp.arange(groups, dtype=jnp.int32)
    forest = jax.vmap(lambda group: random_tree(jax.random.fold_in(key, 1000 + group), LEAVES_DEV))(indices)
    return forest.reshape(BRANCHES)


def draw_top_parents(key, part):
    return random_tree(jax.random.fold_in(key, 3), TOP_BR // 2 + 1)


def draw_tips(key, part):
    states_key, noise_key = jax.random.split(jax.random.fold_in(key, 5))
    observed = jax.random.randint(states_key, (TAXA, SITES), 0, CODONS)
    noise_draw = jax.random.uniform(noise_key, (TAXA, STATES, SITES), jnp.float32)
    observed_hot = (observed[:, None, :] == jnp.arange(STATES)[None, :, None]).astype(jnp.float32)
    return (0.02 + 0.1 * noise_draw + observed_hot).astype(jnp.float32)


def codon_model(key):
    rate_key, freq_key, label_key = jax.random.split(jax.random.fold_in(key, 11), 3)
    raw_rates = jax.random.uniform(rate_key, (CODONS, CODONS), jnp.float32, 0.1, 2.0)
    exchange_rates = (raw_rates + raw_rates.T) / 2.0
    raw_freq = jax.random.uniform(freq_key, (CODONS,), jnp.float32, 0.5, 2.0)
    freq = raw_freq / jnp.sum(raw_freq)
    off_diag = exchange_rates * freq[None, :] * (1.0 - jnp.eye(CODONS, dtype=jnp.float32))
    diag_rates = -jnp.sum(off_diag, axis=1)
    mean_rate = -jnp.sum(freq * diag_rates)
    off_diag = off_diag / mean_rate
    diag_rates = diag_rates / mean_rate
    root_freq_sqrt = jnp.sqrt(freq)
    symmetric = off_diag * root_freq_sqrt[:, None] / root_freq_sqrt[None, :] + jnp.diag(diag_rates)
    symmetric = (symmetric + symmetric.T) / 2.0
    values, vectors = jnp.linalg.eigh(symmetric)
    right = vectors / root_freq_sqrt[:, None]
    left = vectors.T * root_freq_sqrt[None, :]
    label_draw = jax.random.bernoulli(label_key, 0.6, (CODONS, CODONS))
    label_draw = jnp.logical_and(label_draw, label_draw.T).astype(jnp.float32)
    labeled = off_diag * label_draw
    full_right = jnp.eye(STATES, dtype=jnp.float32).at[:CODONS, :CODONS].set(right)
    full_left = jnp.eye(STATES, dtype=jnp.float32).at[:CODONS, :CODONS].set(left)
    full_values = jnp.zeros((STATES,), jnp.float32).at[:CODONS].set(values)
    full_labeled = jnp.zeros((STATES, STATES), jnp.float32).at[:CODONS, :CODONS].set(labeled)
    full_freq = jnp.zeros((STATES,), jnp.float32).at[:CODONS].set(freq)
    return (full_right, full_left, full_values, full_labeled, full_freq)


def draw_eig_vectors(key, part):
    return codon_model(key)[0].astype(jnp.float32)


def draw_eig_inverse(key, part):
    return codon_model(key)[1].astype(jnp.float32)


def draw_eig_values(key, part):
    return codon_model(key)[2].astype(jnp.float32)


def draw_labeled_rates(key, part):
    return codon_model(key)[3].astype(jnp.float32)


def draw_root_freq(key, part):
    return codon_model(key)[4].astype(jnp.float32)


def plant(drawn, own_key, low, top_value):
    longest = drawn.shape.index(max(drawn.shape))
    spots = []
    for shift in (0, 1):
        where = [jax.random.randint(jax.random.fold_in(own_key, axis), (), 0, length) for axis, length in enumerate(drawn.shape)]
        where[longest] = (where[longest] + shift) % drawn.shape[longest]
        spots.append(tuple(where))
    return drawn.at[spots[0]].set(low).at[spots[1]].set(top_value)


def shard_levels(key, extent, cuts, low, largest):
    level, own = 1.0, jax.random.fold_in(key, 6)
    for axis_at, shards_of in cuts:
        draws = jnp.exp(jax.random.uniform(jax.random.fold_in(own, axis_at), (shards_of,), jnp.float32, low / len(cuts), largest / len(cuts)))
        level = level * jnp.repeat(draws, extent[axis_at] // shards_of).reshape([-1 if axis == axis_at else 1 for axis in range(len(extent))])
    return level


def setup_inputs(seed: int = 0) -> dict:
    key_list = jax.random.split(jax.random.key(seed), 12)
    return {
        "tips": draw_tips(jax.random.fold_in(key_list[11], 71), 0),
        "parents": draw_parents(jax.random.fold_in(key_list[11], 71), 0),
        "branch_lengths": jnp.clip(jnp.exp(math.log(0.6) - 3.4011974 * jax.random.uniform(key_list[2], (BRANCHES,), jnp.float32) ** shard_levels(key_list[2], (BRANCHES,), ((0, 64),), -0.2, 0.2)), 0.02, 0.6),
        "top_parents": draw_top_parents(jax.random.fold_in(key_list[11], 71), 0),
        "top_lengths": jnp.clip(jnp.exp(jax.random.uniform(key_list[4], (TOP_BR,), jnp.float32, math.log(0.02), math.log(0.6))), 0.02, 0.6),
        "weights": plant(jax.random.randint(key_list[5], (SITES,), 1, 17), jax.random.fold_in(key_list[5], 1), 1, 16).astype(jnp.int32),
        "eig_vectors": draw_eig_vectors(jax.random.fold_in(key_list[11], 71), 0),
        "eig_inverse": draw_eig_inverse(jax.random.fold_in(key_list[11], 71), 0),
        "eig_values": draw_eig_values(jax.random.fold_in(key_list[11], 71), 0),
        "labeled_rates": draw_labeled_rates(jax.random.fold_in(key_list[11], 71), 0),
        "root_freq": draw_root_freq(jax.random.fold_in(key_list[11], 71), 0),
    }


PRECISE = lax.Precision.HIGHEST

def propagate(eig_vectors, eig_inverse, eig_values, branch, partial_value):
    projected = jnp.dot(eig_inverse, partial_value, precision=PRECISE)
    damping = jnp.exp(eig_values * branch)
    return jnp.dot(eig_vectors, damping[:, None] * projected, precision=PRECISE)

def integrals(eig_values, branch):
    spread = (eig_values[:, None] - eig_values[None, :]) * branch
    near_zero = jnp.abs(spread) < 0.0001
    divisor = jnp.where(near_zero, jnp.ones_like(spread), spread)
    growth = jnp.where(near_zero, 1.0 + spread / 2.0 + spread * spread / 6.0, jnp.expm1(spread) / divisor)
    return branch * jnp.exp(eig_values[None, :] * branch) * growth

def climb_tree(leaf_rows, tree_links, lengths, eig_vectors, eig_inverse, eig_values):
    leaf_count = leaf_rows.shape[0]
    edge_count = tree_links.shape[0]
    inside = jnp.concatenate([leaf_rows, jnp.ones((leaf_count - 1, leaf_rows.shape[1], leaf_rows.shape[2]), jnp.float32)], axis=0)

    def finish(inside, log_scale, position):
        node_row = lax.dynamic_index_in_dim(inside, position, 0, keepdims=False)
        biggest = jnp.max(node_row, axis=0)
        internal = position >= leaf_count
        node_row = jnp.where(internal, node_row / biggest, node_row)
        log_scale = log_scale + jnp.where(internal, jnp.log(biggest), jnp.zeros_like(biggest))
        return (lax.dynamic_update_index_in_dim(inside, node_row, position, 0), log_scale, node_row)

    def visit(position, state_pair):
        inside, log_scale = state_pair
        inside, log_scale, node_row = finish(inside, log_scale, position)
        message = propagate(eig_vectors, eig_inverse, eig_values, lengths[position], node_row)
        parent_node = tree_links[position]
        target = lax.dynamic_index_in_dim(inside, parent_node, 0, keepdims=False) * message
        return (lax.dynamic_update_index_in_dim(inside, target, parent_node, 0), log_scale)
    log_scale = jnp.zeros((leaf_rows.shape[2],), jnp.float32)
    inside, log_scale = lax.fori_loop(0, edge_count, visit, (inside, log_scale))
    inside, log_scale, _ = finish(inside, log_scale, edge_count)
    return (inside, log_scale)

def descend(inside, tree_links, lengths, root_out, weight, eig_vectors, eig_inverse, eig_values, count_basis):
    node_count = inside.shape[0]
    edge_count = node_count - 1
    labels = jnp.arange(node_count, dtype=jnp.int32)
    edges = jnp.arange(edge_count, dtype=jnp.int32)
    member = tree_links[None, :] == labels[:, None]
    child_sum = jnp.sum(jnp.where(member, edges[None, :], 0), axis=1).astype(jnp.int32)
    sibling = (child_sum[tree_links] - edges).astype(jnp.int32)
    outside = jnp.zeros_like(inside).at[node_count - 1].set(root_out)

    def visit(counter, state_pair):
        outside, totals = state_pair
        position = edge_count - 1 - counter
        parent_node = tree_links[position]
        beside = sibling[position]
        branch = lengths[position]
        partner = propagate(eig_vectors, eig_inverse, eig_values, lengths[beside], lax.dynamic_index_in_dim(inside, beside, 0, keepdims=False))
        arriving = lax.dynamic_index_in_dim(outside, parent_node, 0, keepdims=False) * partner
        weighted = jnp.dot(eig_vectors.T, arriving, precision=PRECISE)
        projected = jnp.dot(eig_inverse, lax.dynamic_index_in_dim(inside, position, 0, keepdims=False), precision=PRECISE)
        damping = jnp.exp(eig_values * branch)
        denominator = jnp.sum(weighted * damping[:, None] * projected, axis=0)
        mixed_rows = jnp.dot(count_basis * integrals(eig_values, branch), projected, precision=PRECISE)
        numerator = jnp.sum(weighted * mixed_rows, axis=0)
        pattern_total = jnp.sum(weight * numerator / denominator)
        outward = jnp.dot(eig_inverse.T, damping[:, None] * weighted, precision=PRECISE)
        outward = outward / jnp.max(outward, axis=0)
        outside = lax.dynamic_update_index_in_dim(outside, outward, position, 0)
        return (outside, totals.at[position].set(pattern_total))
    totals = jnp.zeros((edge_count,), jnp.float32)
    return lax.fori_loop(0, edge_count, visit, (outside, totals))

def reference(tips, parents, branch_lengths, top_parents, top_lengths, weights, eig_vectors, eig_inverse, eig_values, labeled_rates, root_freq):
    codon_mask = (jnp.arange(STATES) < CODONS).astype(jnp.float32)
    count_basis = jnp.dot(jnp.dot(eig_inverse, labeled_rates, precision=PRECISE), eig_vectors, precision=PRECISE)
    tip_blocks = tips.reshape(N_LEAF, LEAVES_DEV, STATES, SITES)
    parent_blocks = parents.reshape(N_LEAF, BR_DEV)
    length_blocks = branch_lengths.reshape(N_LEAF, BR_DEV)

    def upward(subtree):
        leaf_rows, tree_links, lengths = subtree
        inside, log_scale = climb_tree(leaf_rows * codon_mask[None, :, None], tree_links, lengths, eig_vectors, eig_inverse, eig_values)
        return (inside[-1], log_scale)
    root_rows, root_logs = lax.map(upward, (tip_blocks, parent_blocks, length_blocks))
    top_inside, top_logs = climb_tree(root_rows, top_parents, top_lengths, eig_vectors, eig_inverse, eig_values)
    weight = weights.astype(jnp.float32)
    likelihood = jnp.sum(root_freq[:, None] * top_inside[-1], axis=0)
    site_loglik = (jnp.log(likelihood) + top_logs + jnp.sum(root_logs, axis=0)) / TAXA
    root_start = jnp.broadcast_to(root_freq[:, None], (STATES, SITES))
    top_outside, top_totals = descend(top_inside, top_parents, top_lengths, root_start, weight, eig_vectors, eig_inverse, eig_values, count_basis)

    def downward(subtree):
        leaf_rows, tree_links, lengths, root_out = subtree
        inside, _ = climb_tree(leaf_rows * codon_mask[None, :, None], tree_links, lengths, eig_vectors, eig_inverse, eig_values)
        _, totals = descend(inside, tree_links, lengths, root_out, weight, eig_vectors, eig_inverse, eig_values, count_basis)
        return totals
    local_totals = lax.map(downward, (tip_blocks, parent_blocks, length_blocks, top_outside[:N_LEAF]))
    weight_total = jnp.sum(weight)
    return (local_totals.reshape(BRANCHES) / weight_total, top_totals / weight_total, site_loglik)
```

```python
import functools

import jax
import jax.numpy as jnp
from jax import lax
from jax.experimental import pallas as pl
from jax.experimental.pallas import tpu as pltpu
from jax.sharding import PartitionSpec as P

CODONS = 61
S = 64
T = 128
LEAVES = 8
LOC = 14
GROUPS = 64
TOP = 126
ROOT = 126
WIN = 4
F32 = jnp.float32
BF16 = jnp.bfloat16
PRECISE = lax.Precision.HIGHEST


def split(u):
    high = u.astype(BF16)
    low = (u - high.astype(F32)).astype(BF16)
    return high, low


def apply(w, u):
    high, low = split(u)
    return jnp.dot(w, jnp.concatenate([high, low, high, low], axis=0), preferred_element_type=F32)


def pack(doubled):
    high, low = split(doubled)
    return jnp.concatenate([high, low], axis=1)


def dot(a, b):
    return jnp.dot(a, b, precision=PRECISE, preferred_element_type=F32)


def growth(x):
    series = 1.0 + x * (1 / 2 + x * (1 / 6 + x * (1 / 24 + x * (1 / 120 + x * (
        1 / 720 + x * (1 / 5040 + x * (1 / 40320)))))))
    small = jnp.abs(x) < 0.5
    safe = jnp.where(small, 1.0, x)
    return jnp.where(small, series, (jnp.exp(x) - 1.0) / safe)


def iota(shape, axis):
    return lax.broadcasted_iota(jnp.int32, shape, axis)


def column(row):
    eye = iota((S, S), 0) == iota((S, S), 1)
    return jnp.sum(jnp.where(eye, row, 0.0), axis=1, keepdims=True)


def biggest(u):
    inside = iota((S, T), 0) < CODONS
    return jnp.max(jnp.where(inside, u, 0.0), axis=0, keepdims=True)


def inverse(row):
    return pltpu.reciprocal(row, approx=True)


def integral_matrix(vectors, inverse_vectors, basis, lam_row, lam_col, t):
    spread = (lam_col - lam_row) * t
    held = basis * (t * jnp.exp(lam_row * t) * growth(spread))
    return dot(dot(vectors, held), jnp.concatenate([inverse_vectors, inverse_vectors], axis=1))


def local_children(parents, node):
    late, early = jnp.int32(0), jnp.int32(0)
    for c in range(LOC):
        hit = parents[c] == node
        early = jnp.where(hit, late, early)
        late = jnp.where(hit, c, late)
    return late, early


def prepare(parents, lengths, top_lengths, tips, vectors, inverse_vectors, lam, rates,
            sent, w_top, w_loc, m_loc, y_loc, expo, x_int):
    me = lax.axis_index("leaf")
    lam_row = lam[...]
    lam_col = column(lam_row)
    lam2 = jnp.concatenate([lam_row, lam_row], axis=1)
    used = iota((S, S), 0) < CODONS
    right = jnp.where(used, vectors[...], 0.0)
    left = inverse_vectors[...]
    right2 = jnp.concatenate([right, right], axis=1)
    left2 = jnp.concatenate([left, left], axis=1)
    left_high, left_low = split(left2)
    left_stack = jnp.concatenate([left_high, left_low, left_high, left_low], axis=0)
    r2, c2 = iota((S, T), 0), iota((S, T), 1)
    eye2 = jnp.where((r2 < CODONS) & ((r2 == c2) | (r2 + S == c2)), 1.0, 0.0)

    def branch(t):
        x = lam2 * t
        scaled = right2 * (x * growth(x))
        return pack(eye2 + jnp.dot(pack(scaled), left_stack, preferred_element_type=F32))

    for c in range(LOC):
        w_loc[c] = branch(lengths[c])
    w_loc[LOC] = branch(top_lengths[me])

    for c in range(LEAVES):
        m_loc[c] = apply(w_loc[c], tips[c])
    factors = []
    for n in range(LEAVES, LOC + 1):
        a, b = local_children(parents, n)
        u = m_loc[a] * m_loc[b]
        r = inverse(biggest(u))
        factors.append(r)
        x_int[n - LEAVES] = u * r
        y = apply(w_loc[n], u) * r
        if n < LOC:
            m_loc[n] = y
        else:
            logs = -jnp.sum(jnp.log(jnp.concatenate(factors, axis=0)), axis=0, keepdims=True)
            sent[...] = jnp.where(iota((S, T), 0) == S - 1, logs, y)

    basis = dot(dot(left, rates[...]), right)
    for c in range(LOC + 1):
        t = lengths[c] if c < LOC else top_lengths[me]
        n_c = integral_matrix(right, left, basis, lam_row, lam_col, t)
        y_loc[c] = apply(pack(n_c), tips[c] if c < LEAVES else x_int[c - LEAVES])

    def top_branch(i, _):
        w_top[i] = branch(top_lengths[GROUPS + i])
        return 0

    lax.fori_loop(0, TOP - GROUPS, top_branch, 0)
    for i in range(TOP - GROUPS, TOP - GROUPS + WIN):
        w_top[i] = jnp.zeros((S, 256), BF16)


def joining(top_parents, parents, top_lengths, gathered, w_top, w_loc, m_loc, y_loc, weights, vectors,
            inverse_vectors, lam, rates, freq, out, late, early, path, msg, factor, arrs, o_loc, rows, sem):
    copy = pltpu.make_async_copy(gathered, msg.at[pl.ds(0, GROUPS)], sem)
    copy.start()
    me = lax.axis_index("leaf")

    def link(c, _):
        p = top_parents[c]
        early[p] = late[p]
        late[p] = c
        return 0

    for i in range(GROUPS, ROOT + 1 + WIN):
        late[i] = 0
        early[i] = 0
    lax.fori_loop(0, TOP, link, 0, unroll=2)
    factor[...] = jnp.ones((72, T), F32)
    copy.wait()
    local_logs = msg[0, pl.ds(S - 1, 1)]
    for g in range(1, GROUPS):
        local_logs += msg[g, pl.ds(S - 1, 1)]

    def climb(n):
        done = []
        fits = True
        steps = jnp.int32(1)
        for j in range(WIN):
            a, b = late[n + j], early[n + j]
            if j:
                fits = fits & (a < n)
                steps = steps + fits.astype(jnp.int32)
            u = msg[a] * msg[b]
            y = apply(w_top[n + j - GROUPS], u)
            r = inverse(biggest(u))
            done.append((y * r, r))
        for j, (y, r) in enumerate(done):
            msg[n + j] = y
            factor[pl.ds(n + j - GROUPS, 1)] = r
        return n + steps

    lax.while_loop(lambda n: n < ROOT, climb, jnp.int32(GROUPS))

    freq_col = column(freq[...])
    root_u = msg[late[ROOT]] * msg[early[ROOT]]
    likelihood = jnp.sum(freq_col * root_u, axis=0, keepdims=True)
    row = iota((72, T), 0)
    top_logs = -jnp.sum(jnp.log(jnp.where(row < TOP - GROUPS, factor[...], 1.0)), axis=0, keepdims=True)
    loglik = (jnp.log(likelihood) + top_logs + local_logs) * (1.0 / (GROUPS * LEAVES))

    def walk(state):
        c, depth, mine, at = state
        path[depth] = c
        p = top_parents[c]
        found = (mine < 0) & (late[p] == c)
        return (p, depth + 1, jnp.where(found, p, mine), jnp.where(found, depth + 1, at))

    _, depth, mine, at = lax.while_loop(
        lambda state: state[0] != ROOT, walk, (me, jnp.int32(0), jnp.int32(-1), jnp.int32(0)))
    counted = (mine >= 0) & (mine < ROOT)
    node = jnp.where(counted, mine, GROUPS)
    at = jnp.where(counted, at, 0)

    def step_down(i, o):
        k = depth - 1 - i
        c = path[k]
        p = top_parents[c]
        arriving = o * msg[late[p] + early[p] - c]
        arrs[k] = arriving
        w = w_top[c - GROUPS]
        return apply(w, arriving) * inverse(biggest(arriving))

    o = lax.fori_loop(0, depth - 1, step_down, jnp.ones((S, T), F32))
    p = top_parents[me]
    arriving = o * msg[late[p] + early[p] - me]
    arrs[0] = arriving
    o_loc[LOC - LEAVES] = apply(w_loc[LOC], arriving) * inverse(biggest(arriving))

    def ratio(slot, arriving, message, y):
        weighted = freq_col * arriving
        rows[0, pl.ds(slot, 1)] = jnp.sum(weighted * y, axis=0, keepdims=True)
        rows[1, pl.ds(slot, 1)] = jnp.sum(weighted * message, axis=0, keepdims=True)

    rows[...] = jnp.ones((2, 24, T), F32)
    ratio(16, arriving, msg[me], y_loc[LOC])
    lam_row = lam[...]
    used = iota((S, S), 0) < CODONS
    right = jnp.where(used, vectors[...], 0.0)
    left = inverse_vectors[...]
    basis = dot(dot(left, rates[...]), right)
    n_c = integral_matrix(right, left, basis, lam_row, column(lam_row), top_lengths[node])
    u = msg[late[node]] * msg[early[node]]
    ratio(17, arrs[at], msg[node], apply(pack(n_c), u) * factor[pl.ds(node - GROUPS, 1)])

    for c in range(LOC - 1, -1, -1):
        p = parents[c]
        sibling = jnp.int32(0)
        for other in range(LOC):
            if other != c:
                sibling = jnp.where(parents[other] == p, other, sibling)
        arriving = o_loc[p - LEAVES] * m_loc[sibling]
        if c >= LEAVES:
            o_loc[c - LEAVES] = apply(w_loc[c], arriving) * inverse(biggest(arriving))
        ratio(c, arriving, m_loc[c], y_loc[c])

    weight = weights[...].astype(F32)
    expected = weight * rows[0] / rows[1]
    slot = iota((24, T), 0)
    expected = jnp.where(slot == LOC, weight, expected)
    sums = lax.dot_general(jnp.ones((8, T), F32), expected, (((1,), (1,)), ((), ())),
                           precision=PRECISE, preferred_element_type=F32)
    lane = iota((1, T), 1)
    own = sums[0:1, 16:17]
    inner = sums[0:1, 17:18]
    top_row = jnp.where(lane == me, own, 0.0) + jnp.where((lane == node) & counted, inner, 0.0)
    out[...] = jnp.zeros((8, T), F32)
    out[pl.ds(0, 1), pl.ds(0, 24)] = sums[0:1]
    out[pl.ds(1, 1)] = top_row
    out[pl.ds(2, 1)] = loglik


def on_device(tips, parents, branch_lengths, top_parents, top_lengths, weights, eig_vectors,
              eig_inverse, eig_values, labeled_rates, root_freq):
    smem = pl.BlockSpec(memory_space=pltpu.SMEM)
    vmem = pl.BlockSpec(memory_space=pltpu.VMEM)
    params = pltpu.CompilerParams(vmem_limit_bytes=40 << 20)
    lam = eig_values.reshape(1, S)
    freq = root_freq.reshape(1, S)
    sent, w_top, w_loc, m_loc, y_loc = pl.pallas_call(
        prepare,
        out_shape=(
            jax.ShapeDtypeStruct((S, T), F32),
            jax.ShapeDtypeStruct((TOP - GROUPS + WIN, S, 256), BF16),
            jax.ShapeDtypeStruct((LOC + 1, S, 256), BF16),
            jax.ShapeDtypeStruct((LOC, S, T), F32),
            jax.ShapeDtypeStruct((LOC + 1, S, T), F32),
        ),
        in_specs=[smem] * 3 + [vmem] * 5,
        out_specs=(vmem,) * 5,
        scratch_shapes=[pltpu.VMEM((8, T), F32), pltpu.VMEM((8, S, T), F32)],
        compiler_params=params,
        name="prepare",
    )(parents, branch_lengths, top_lengths, tips, eig_vectors, eig_inverse, lam, labeled_rates)
    gathered = lax.all_gather(sent, "leaf")
    out = pl.pallas_call(
        joining,
        out_shape=jax.ShapeDtypeStruct((8, T), F32),
        in_specs=[smem] * 3 + [pl.BlockSpec(memory_space=pl.ANY)] + [vmem] * 10,
        out_specs=vmem,
        scratch_shapes=[
            pltpu.SMEM((136,), jnp.int32),
            pltpu.SMEM((136,), jnp.int32),
            pltpu.SMEM((64,), jnp.int32),
            pltpu.VMEM((ROOT + 1 + WIN, S, T), F32),
            pltpu.VMEM((72, T), F32),
            pltpu.VMEM((GROUPS, S, T), F32),
            pltpu.VMEM((8, S, T), F32),
            pltpu.VMEM((2, 24, T), F32),
            pltpu.SemaphoreType.DMA,
        ],
        compiler_params=params,
        name="joining",
    )(top_parents, parents, top_lengths, gathered, w_top, w_loc, m_loc, y_loc, weights.reshape(1, T),
      eig_vectors, eig_inverse, lam, labeled_rates, freq)
    local_sum = lax.psum(out[0, :LOC + 1], "site")
    top_sum = lax.psum(out[1], ("leaf", "site"))
    total = local_sum[LOC]
    return local_sum[:LOC] / total, top_sum[:TOP] / total, out[2]


def solution(mesh):
    placed = (P("leaf", None, "site"), P("leaf"), P("leaf"), P(), P(), P("site"), P(), P(), P(), P(), P())
    return jax.shard_map(
        on_device,
        mesh=mesh,
        in_specs=placed,
        out_specs=(P("leaf"), P(), P("site")),
        check_vma=False,
    )
```

```python
import functools

import jax
import jax.numpy as jnp
from jax import lax
from jax.experimental import pallas as pl
from jax.experimental.pallas import tpu as pltpu
from jax.sharding import PartitionSpec as P

CODONS = 61
S = 64
T = 128
LEAVES = 8
LOC = 14
GROUPS = 64
TOP = 126
ROOT = 126
WIN = 4
NX, NZ, NY = 4, 8, 8
CUT = 40
HOPS = ((1, 4), (-1, 3))
F32 = jnp.float32
BF16 = jnp.bfloat16
PRECISE = lax.Precision.HIGHEST
MESH = pl.DeviceIdType.MESH


def split(u):
    high = u.astype(BF16)
    low = (u - high.astype(F32)).astype(BF16)
    return high, low


def apply(w, u):
    high, low = split(u)
    return jnp.dot(w, jnp.concatenate([high, low, high, low], axis=0), preferred_element_type=F32)


def pack(doubled):
    high, low = split(doubled)
    return jnp.concatenate([high, low], axis=1)


def double(a):
    return jnp.concatenate([a, a], axis=1)


def dot(a, b):
    return jnp.dot(a, b, precision=PRECISE, preferred_element_type=F32)


def growth(x):
    series = 1.0 + x * (1 / 2 + x * (1 / 6 + x * (1 / 24 + x * (1 / 120 + x * (
        1 / 720 + x * (1 / 5040 + x * (1 / 40320)))))))
    small = jnp.abs(x) < 0.5
    safe = jnp.where(small, 1.0, x)
    return jnp.where(small, series, (jnp.exp(x) - 1.0) / safe)


def iota(shape, axis):
    return lax.broadcasted_iota(jnp.int32, shape, axis)


def column(row):
    n = row.shape[1]
    eye = iota((n, n), 0) == iota((n, n), 1)
    return jnp.sum(jnp.where(eye, row, jnp.zeros_like(row)), axis=1, keepdims=True)


def biggest(u):
    used = iota((S, T), 0) < CODONS
    return jnp.max(jnp.where(used, u, 0.0), axis=0, keepdims=True)


def inverse(row):
    return pltpu.reciprocal(row, approx=True)


def held_integrals(basis2, lam2, lam_col, t):
    spread = (lam_col - lam2) * t
    return pack(basis2 * (t * jnp.exp(lam2 * t) * growth(spread)))


def local_children(parents, node):
    late, early = jnp.int32(0), jnp.int32(0)
    for c in range(LOC):
        hit = parents[c] == node
        early = jnp.where(hit, late, early)
        late = jnp.where(hit, c, late)
    return late, early


def slot_of(x, z, c):
    return c * (NX * NZ) + z * NX + x


def prepare(parents_h, lengths_h, top_lengths_h, top_parents_h, tips_h, vectors_h, inverse_h, lam_h, rates_h, freq_h,
            msg, w_top, w_loc, m_loc, y_loc, links, eig_w, inv_w, basis_out, lam_out, freq_out,
            parents, lengths, top_lengths, top_parents, tips, vectors, inverse_vectors, lam, rates, freq, x_int,
            in_sem, send_sem, recv_sem):
    me = lax.axis_index("leaf")
    site = lax.axis_index("site")
    core = lax.rem(me, 2)
    z = lax.rem(me // 2, NZ)
    x = me // (2 * NZ)

    loads = [pltpu.make_async_copy(src, dst, in_sem.at[i]) for i, (src, dst) in enumerate((
        (vectors_h, vectors), (inverse_h, inverse_vectors), (lam_h, lam), (lengths_h, lengths),
        (top_lengths_h, top_lengths), (tips_h, tips), (parents_h, parents), (rates_h, rates),
        (top_parents_h, top_parents), (freq_h, freq)))]
    for load in loads:
        load.start()

    def device(dx, dz, dc):
        nx, nz = lax.rem(x + dx + NX, NX), lax.rem(z + dz + NZ, NZ)
        nc = 1 - core if dc else core
        return ((nx * NZ + nz) * 2 + nc, site)

    x_peers = [(dx, 0, 0) for dx in (1, 2, 3)]
    partners = x_peers + [(0, 1, 0), (0, -1, 0), (0, 0, 1)]
    barrier = pltpu.get_barrier_semaphore()
    for partner in partners:
        pl.semaphore_signal(barrier, inc=1, device_id=device(*partner), device_id_type=MESH)

    for load in loads[:5]:
        load.wait()
    lam_row = lam[...]
    lam_col = column(lam_row)
    lam2 = double(lam_row)
    used = iota((S, S), 0) < CODONS
    right = jnp.where(used, vectors[...], 0.0)
    left = inverse_vectors[...]
    right2 = double(right)
    left_high, left_low = split(double(left))
    left_stack = jnp.concatenate([left_high, left_low, left_high, left_low], axis=0)
    r2, c2 = iota((S, T), 0), iota((S, T), 1)
    eye2 = jnp.where((r2 < CODONS) & ((r2 == c2) | (r2 + S == c2)), 1.0, 0.0)

    def branches(ts):
        scaled = []
        for t in ts:
            arg = lam2 * t
            scaled.append(pack(right2 * (arg * growth(arg))))
        result = jnp.dot(jnp.concatenate(scaled, axis=0), left_stack, preferred_element_type=F32)
        return [pack(eye2 + result[S * i:S * (i + 1)]) for i in range(len(ts))]

    for c, w in enumerate(branches([lengths[c] for c in range(LOC)] + [top_lengths[me]])):
        w_loc[c] = w

    loads[5].wait()
    loads[6].wait()
    for c in range(LEAVES):
        m_loc[c] = apply(w_loc[c], tips[c])
    factors = []
    for n in range(LEAVES, LOC + 1):
        a, b = local_children(parents, n)
        u = m_loc[a] * m_loc[b]
        r = inverse(biggest(u))
        factors.append(r)
        x_int[n - LEAVES] = u * r
        y = apply(w_loc[n], u) * r
        if n < LOC:
            m_loc[n] = y
        else:
            logs = -jnp.sum(jnp.log(jnp.concatenate(factors, axis=0)), axis=0, keepdims=True)
            msg[slot_of(x, z, core)] = jnp.where(iota((S, T), 0) == S - 1, logs, y)
    pl.semaphore_wait(barrier, len(partners))

    counter = [0]

    def own_piece(xs, zs, rows):
        if xs is None:
            return msg.at[pl.ds(slot_of(0, zs, core), NX), rows]
        return msg.at[slot_of(xs, zs, core), rows]

    def other_piece(zs, rows):
        return msg.at[pl.ds(slot_of(0, zs, 1 - core), NX), rows]

    started = []

    def send(piece, where, arriving):
        k = counter[0]
        counter[0] += 1
        copy = pltpu.make_async_remote_copy(src_ref=piece, dst_ref=piece, send_sem=send_sem.at[k],
                                            recv_sem=recv_sem.at[k], device_id=device(*where), device_id_type=MESH)
        copy.start()
        started.append(copy)
        incoming = pltpu.make_async_remote_copy(src_ref=arriving, dst_ref=arriving, send_sem=send_sem.at[k],
                                                recv_sem=recv_sem.at[k], device_id=device(*where), device_id_type=MESH)
        return incoming

    first, second = pl.ds(0, CUT), pl.ds(CUT, S - CUT)

    def at_z(dz):
        return lax.rem(z + dz + NZ, NZ)

    def at_x(dx):
        return lax.rem(x + dx + NX, NX)

    def spread_x(dz):
        return [send(own_piece(x, at_z(dz), first), (dx, 0, 0), own_piece(at_x(-dx), at_z(dz), first))
                for dx in (1, 2, 3)]

    def cross(dz, rows):
        return send(own_piece(None, at_z(dz), rows), (0, 0, 1), other_piece(at_z(dz), rows))

    def hop_first(direction, h):
        return send(own_piece(x, at_z(-direction * (h - 1)), first), (0, direction, 0),
                    own_piece(x, at_z(-direction * h), first))

    def hop_second(direction, h):
        return send(own_piece(None, at_z(-direction * (h - 1)), second), (0, direction, 0),
                    own_piece(None, at_z(-direction * h), second))

    def work(stage):
        if stage == 0:
            loads[7].wait()
            loads[8].wait()
            loads[9].wait()
            parent_col = column(top_parents[...])
            child = iota((TOP, T), 0)
            hit = parent_col == iota((TOP, T), 1)
            late = jnp.max(jnp.where(hit, child, 0), axis=0, keepdims=True)
            early = jnp.min(jnp.where(hit, child, TOP), axis=0, keepdims=True)
            pair = jnp.concatenate([late, early, jnp.zeros((6, T), jnp.int32)], axis=0)
            slots = (pair & 1) * (NX * NZ) + ((pair >> 1) & (NZ - 1)) * NX + (pair >> 4)
            pair = jnp.where(pair < GROUPS, slots, pair)
            lane = iota((8, T), 1)
            links[...] = jnp.where((lane >= GROUPS) & (lane <= ROOT), pair, 0)
            freq_out[...] = jnp.broadcast_to(column(freq[...]), (S, T))
            lam_out[...] = jnp.broadcast_to(lam2, (8, T))
            basis_out[...] = double(dot(dot(left, rates[...]), right))
            eig_w[...] = pack(right2)
            inv_w[...] = pack(double(left))
        elif stage <= 4:
            per = 4
            for c in range((stage - 1) * per, min(stage * per, LOC + 1)):
                t = lengths[c] if c < LOC else top_lengths[me]
                v = apply(inv_w[...], tips[c] if c < LEAVES else x_int[c - LEAVES])
                y_loc[c] = apply(eig_w[...], apply(held_integrals(basis_out[...], lam2, lam_col, t), v))
        else:
            lo, hi = ((0, 4), (4, 8))[stage - 5]

            def some(i, _):
                for j, w in enumerate(branches([top_lengths[jnp.minimum(GROUPS + i * 8 + j, TOP - 1)] for j in range(8)])):
                    w_top[i * 8 + j] = w
                return 0

            lax.fori_loop(lo, hi, some, 0)

    x_second = [send(own_piece(x, z, second), (dx, 0, 0), own_piece(at_x(-dx), z, second)) for dx in (1, 2, 3)]
    z_first = {d: hop_first(d, 1) for d, _ in HOPS}
    spreads = [(0, spread_x(0))]
    crossed = []
    work(0)
    for incoming in x_second:
        incoming.wait_recv()
    z_second = {d: hop_second(d, 1) for d, _ in HOPS}
    crossed.append(cross(0, second))
    for h in range(1, 5):
        work(h)
        for d, most in HOPS:
            if h > most:
                continue
            z_first[d].wait_recv()
            if h < most:
                z_first[d] = hop_first(d, h + 1)
            spreads.append((-d * h, spread_x(-d * h)))
        for d, most in HOPS:
            if h > most:
                continue
            z_second[d].wait_recv()
            if h < most:
                z_second[d] = hop_second(d, h + 1)
            crossed.append(cross(-d * h, second))
        ready, spreads = spreads[:-2], spreads[-2:]
        for dz, incoming in ready:
            for one in incoming:
                one.wait_recv()
            crossed.append(cross(dz, first))
    work(5)
    for dz, incoming in spreads:
        for one in incoming:
            one.wait_recv()
        crossed.append(cross(dz, first))
    work(6)
    for one in crossed:
        one.wait_recv()
    for one in started:
        one.wait_send()


COPIES = 3 + 7 + 24 + 7 + 16


def joining(top_parents_h, parents_h, top_lengths_h, weights_h, links, msg_in, w_top, w_loc, m_loc, y_loc,
            eig_w, inv_w, basis, lam, freq, out, msg,
            top_parents, parents, top_lengths, weights, path, factor, arrs, o_loc, rows, sem):
    del msg_in
    loads = [pltpu.make_async_copy(src, dst, sem.at[i]) for i, (src, dst) in enumerate((
        (top_parents_h, top_parents), (parents_h, parents), (top_lengths_h, top_lengths), (weights_h, weights)))]
    for load in loads:
        load.start()
    me = lax.axis_index("leaf")
    slot = slot_of(me // (2 * NZ), lax.rem(me // 2, NZ), lax.rem(me, 2))
    factor[...] = jnp.ones((72, T), F32)
    local_logs = msg[0, pl.ds(S - 1, 1)]
    for g in range(1, GROUPS):
        local_logs += msg[g, pl.ds(S - 1, 1)]

    def late(n):
        return links[0, n]

    def early(n):
        return links[1, n]

    def climb(n):
        done = []
        fits = True
        steps = jnp.int32(1)
        for j in range(WIN):
            k = jnp.minimum(n + j, T - 1) if j > 1 else n + j
            a, b = late(k), early(k)
            if j:
                fits = fits & (a < n)
                steps = steps + fits.astype(jnp.int32)
            u = msg[a] * msg[b]
            y = apply(w_top[jnp.minimum(k, ROOT) - GROUPS], u)
            r = inverse(biggest(u))
            done.append((y * r, r))
        for j, (y, r) in enumerate(done):
            msg[n + j] = y
            factor[pl.ds(n + j - GROUPS, 1)] = r
        return n + steps

    lax.while_loop(lambda n: n < ROOT, climb, jnp.int32(GROUPS))

    freq_col = freq[...]
    root_u = msg[late(ROOT)] * msg[early(ROOT)]
    likelihood = jnp.sum(freq_col * root_u, axis=0, keepdims=True)
    row = iota((72, T), 0)
    top_logs = -jnp.sum(jnp.log(jnp.where(row < TOP - GROUPS, factor[...], 1.0)), axis=0, keepdims=True)
    loglik = (jnp.log(likelihood) + top_logs + local_logs) * (1.0 / (GROUPS * LEAVES))
    for load in loads:
        load.wait()

    def walk(state):
        c, depth, mine, at = state
        path[depth] = c
        p = top_parents[jnp.where(depth == 0, me, c)]
        found = (mine < 0) & (late(p) == c)
        return (p, depth + 1, jnp.where(found, p, mine), jnp.where(found, depth + 1, at))

    _, depth, mine, at = lax.while_loop(
        lambda state: state[0] != ROOT, walk, (slot, jnp.int32(0), jnp.int32(-1), jnp.int32(0)))
    counted = (mine >= 0) & (mine < ROOT)
    node = jnp.where(counted, mine, GROUPS)
    at = jnp.where(counted, at, 0)

    def step_down(i, o):
        k = depth - 1 - i
        c = path[k]
        p = top_parents[c]
        arriving = o * msg[late(p) + early(p) - c]
        arrs[k] = arriving
        return apply(w_top[c - GROUPS], arriving) * inverse(biggest(arriving))

    o = lax.fori_loop(0, depth - 1, step_down, jnp.ones((S, T), F32))
    p = top_parents[me]
    arriving = o * msg[late(p) + early(p) - slot]
    arrs[0] = arriving
    o_loc[LOC - LEAVES] = apply(w_loc[LOC], arriving) * inverse(biggest(arriving))

    def ratio(place, arriving, message, y):
        weighted = freq_col * arriving
        rows[0, pl.ds(place, 1)] = jnp.sum(weighted * y, axis=0, keepdims=True)
        rows[1, pl.ds(place, 1)] = jnp.sum(weighted * message, axis=0, keepdims=True)

    rows[...] = jnp.ones((2, 24, T), F32)
    ratio(16, arriving, msg[slot], y_loc[LOC])
    lam2 = lam[0:1]
    v = apply(inv_w[...], msg[late(node)] * msg[early(node)]) * factor[pl.ds(node - GROUPS, 1)]
    y = apply(eig_w[...], apply(held_integrals(basis[...], lam2, column(lam2[:, :S]), top_lengths[node]), v))
    ratio(17, arrs[at], msg[node], y)

    for c in range(LOC - 1, -1, -1):
        p = parents[c]
        sibling = jnp.int32(0)
        for other in range(LOC):
            if other != c:
                sibling = jnp.where(parents[other] == p, other, sibling)
        arriving = o_loc[p - LEAVES] * m_loc[sibling]
        if c >= LEAVES:
            o_loc[c - LEAVES] = apply(w_loc[c], arriving) * inverse(biggest(arriving))
        ratio(c, arriving, m_loc[c], y_loc[c])

    weight = weights[...].astype(F32)
    expected = weight * rows[0] / rows[1]
    place = iota((24, T), 0)
    expected = jnp.where(place == LOC, weight, expected)
    sums = lax.dot_general(jnp.ones((8, T), F32), expected, (((1,), (1,)), ((), ())),
                           precision=PRECISE, preferred_element_type=F32)
    lane = iota((1, T), 1)
    own = sums[0:1, 16:17]
    inner = sums[0:1, 17:18]
    top_row = jnp.where(lane == me, own, 0.0) + jnp.where((lane == node) & counted, inner, 0.0)
    out[...] = jnp.zeros((8, T), F32)
    out[pl.ds(0, 1), pl.ds(0, 24)] = sums[0:1]
    out[pl.ds(1, 1)] = top_row
    out[pl.ds(2, 1)] = loglik


def reduce(mine, out, near, partial, far, send_sem, recv_sem):
    me = lax.axis_index("leaf")
    y = lax.axis_index("site")
    ny = lax.axis_size("site")
    core = lax.rem(me, 2)
    z = lax.rem(me // 2, NZ)
    x = me // (2 * NZ)
    nears = [(dy, dc) for dy in range(ny) for dc in (0, 1) if (dy, dc) != (0, 0)]
    fars = [(dx, dz) for dx in range(NX) for dz in range(NZ) if (dx, dz) != (0, 0)]

    def near_at(dy, dc):
        return lax.rem(y + dy + ny, ny), (1 - core if dc else core)

    def far_at(dx, dz):
        return lax.rem(x + dx + NX, NX), lax.rem(z + dz + NZ, NZ)

    def near_device(dy, dc):
        ty, tc = near_at(dy, dc)
        return ((x * NZ + z) * 2 + tc, ty)

    def far_device(dx, dz):
        tx, tz = far_at(dx, dz)
        return ((tx * NZ + tz) * 2 + core, y)

    barrier = pltpu.get_barrier_semaphore()
    for where in nears:
        pl.semaphore_signal(barrier, inc=1, device_id=near_device(*where), device_id_type=MESH)
    for where in fars:
        pl.semaphore_signal(barrier, inc=1, device_id=far_device(*where), device_id_type=MESH)
    pl.semaphore_wait(barrier, len(nears) + len(fars))

    def near_slot(ty, tc):
        return ty * 2 + tc

    near[near_slot(y, core)] = mine[...]
    copies = []
    arrivals = []
    for k, (dy, dc) in enumerate(nears):
        here = near.at[near_slot(y, core)]
        copy = pltpu.make_async_remote_copy(src_ref=mine, dst_ref=here, send_sem=send_sem.at[k],
                                            recv_sem=recv_sem.at[k], device_id=near_device(dy, dc), device_id_type=MESH)
        copy.start()
        copies.append(copy)
        there = near.at[near_slot(*near_at(-dy, dc))]
        arrivals.append(pltpu.make_async_remote_copy(
            src_ref=there, dst_ref=there, send_sem=send_sem.at[k], recv_sem=recv_sem.at[k],
            device_id=near_device(dy, dc), device_id_type=MESH))
    for arrival in arrivals:
        arrival.wait_recv()
    local = near[core]
    top = near[0] + near[1]
    for i in range(1, ny):
        local = local + near[2 * i + core]
        top = top + (near[2 * i] + near[2 * i + 1])
    partial[...] = top
    far[x * NZ + z] = top
    base = len(nears)
    arrivals = []
    for k, (dx, dz) in enumerate(fars):
        copy = pltpu.make_async_remote_copy(src_ref=partial, dst_ref=far.at[x * NZ + z], send_sem=send_sem.at[base + k],
                                            recv_sem=recv_sem.at[base + k], device_id=far_device(dx, dz), device_id_type=MESH)
        copy.start()
        copies.append(copy)
        tx, tz = far_at(-dx, -dz)
        there = far.at[tx * NZ + tz]
        arrivals.append(pltpu.make_async_remote_copy(
            src_ref=there, dst_ref=there, send_sem=send_sem.at[base + k], recv_sem=recv_sem.at[base + k],
            device_id=far_device(dx, dz), device_id_type=MESH))
    for arrival in arrivals:
        arrival.wait_recv()
    top = far[0]
    for i in range(1, NX * NZ):
        top = top + far[i]
    total = local[0:1, LOC:LOC + 1]
    out[...] = mine[...]
    out[pl.ds(0, 1)] = local[0:1] / total
    out[pl.ds(1, 1)] = top[1:2] / total
    for copy in copies:
        copy.wait_send()


def on_device(tips, parents, branch_lengths, top_parents, top_lengths, weights, eig_vectors,
              eig_inverse, eig_values, labeled_rates, root_freq):
    hbm = pl.BlockSpec(memory_space=pltpu.HBM)
    smem = pl.BlockSpec(memory_space=pltpu.SMEM)
    vmem = pl.BlockSpec(memory_space=pltpu.VMEM)
    shape = jax.ShapeDtypeStruct
    msg, *made = pl.pallas_call(
        prepare,
        out_shape=(
            shape((ROOT + 1 + WIN, S, T), F32),
            shape((GROUPS, S, 256), BF16),
            shape((LOC + 1, S, 256), BF16),
            shape((LOC, S, T), F32),
            shape((LOC + 1, S, T), F32),
            shape((8, T), jnp.int32),
            shape((S, 256), BF16),
            shape((S, 256), BF16),
            shape((S, T), F32),
            shape((8, T), F32),
            shape((S, T), F32),
        ),
        in_specs=[hbm] * 10,
        out_specs=(vmem,) * 11,
        scratch_shapes=[
            pltpu.SMEM((LOC,), jnp.int32),
            pltpu.SMEM((LOC,), F32),
            pltpu.SMEM((TOP,), F32),
            pltpu.VMEM((1, TOP), jnp.int32),
            pltpu.VMEM((LEAVES, S, T), F32),
            pltpu.VMEM((S, S), F32),
            pltpu.VMEM((S, S), F32),
            pltpu.VMEM((1, S), F32),
            pltpu.VMEM((S, S), F32),
            pltpu.VMEM((1, S), F32),
            pltpu.VMEM((8, S, T), F32),
            pltpu.SemaphoreType.DMA((10,)),
            pltpu.SemaphoreType.DMA((COPIES,)),
            pltpu.SemaphoreType.DMA((COPIES,)),
        ],
        compiler_params=pltpu.CompilerParams(vmem_limit_bytes=40 << 20, collective_id=0, has_side_effects=True),
        name="prepare",
    )(parents, branch_lengths, top_lengths, top_parents.reshape(1, TOP), tips, eig_vectors, eig_inverse,
      eig_values.reshape(1, S), labeled_rates, root_freq.reshape(1, S))
    w_top, w_loc, m_loc, y_loc, links, eig_w, inv_w, basis, lam, freq = made
    red, _ = pl.pallas_call(
        joining,
        out_shape=(shape((8, T), F32), shape(msg.shape, F32)),
        in_specs=[hbm] * 4 + [smem] + [vmem] * 10,
        out_specs=(vmem, vmem),
        input_output_aliases={5: 1},
        scratch_shapes=[
            pltpu.SMEM((TOP,), jnp.int32),
            pltpu.SMEM((LOC,), jnp.int32),
            pltpu.SMEM((TOP,), F32),
            pltpu.VMEM((1, T), jnp.int32),
            pltpu.SMEM((64,), jnp.int32),
            pltpu.VMEM((72, T), F32),
            pltpu.VMEM((GROUPS, S, T), F32),
            pltpu.VMEM((8, S, T), F32),
            pltpu.VMEM((2, 24, T), F32),
            pltpu.SemaphoreType.DMA((4,)),
        ],
        compiler_params=pltpu.CompilerParams(vmem_limit_bytes=40 << 20),
        name="joining",
    )(top_parents, parents, top_lengths, weights.reshape(1, T), links, msg, w_top, w_loc, m_loc, y_loc,
      eig_w, inv_w, basis, lam, freq)
    ny = lax.axis_size("site")
    count = 2 * ny - 1 + NX * NZ - 1
    out = pl.pallas_call(
        reduce,
        out_shape=shape((8, T), F32),
        in_specs=[vmem],
        out_specs=vmem,
        scratch_shapes=[
            pltpu.VMEM((2 * ny, 8, T), F32),
            pltpu.VMEM((8, T), F32),
            pltpu.VMEM((NX * NZ, 8, T), F32),
            pltpu.SemaphoreType.DMA((count,)),
            pltpu.SemaphoreType.DMA((count,)),
        ],
        compiler_params=pltpu.CompilerParams(collective_id=1, has_side_effects=True),
        name="reduce",
    )(red)
    return out[0, :LOC], out[1, :TOP], out[2]


def solution(mesh):
    placed = (P("leaf", None, "site"), P("leaf"), P("leaf"), P(), P(), P("site"), P(), P(), P(), P(), P())
    return jax.shard_map(
        on_device,
        mesh=mesh,
        in_specs=placed,
        out_specs=(P("leaf"), P(), P("site")),
        check_vma=False,
    )
```

```python
import functools

import jax
import jax.numpy as jnp
from jax import lax
from jax.experimental import pallas as pl
from jax.experimental.pallas import tpu as pltpu
from jax.sharding import PartitionSpec as P

CODONS = 61
S = 64
T = 128
LEAVES = 8
LOC = 14
GROUPS = 64
TOP = 126
ROOT = 126
WIN = 4
F32 = jnp.float32
BF16 = jnp.bfloat16
PRECISE = lax.Precision.HIGHEST
NX, NZ = 4, 8
MESH = pl.DeviceIdType.MESH


def split(u):
    high = u.astype(BF16)
    low = (u - high.astype(F32)).astype(BF16)
    return high, low


def apply(w, u):
    high, low = split(u)
    return jnp.dot(w, jnp.concatenate([high, low, high, low], axis=0), preferred_element_type=F32)


def pack(doubled):
    high, low = split(doubled)
    return jnp.concatenate([high, low], axis=1)


def double(a):
    return jnp.concatenate([a, a], axis=1)


def dot(a, b):
    return jnp.dot(a, b, precision=PRECISE, preferred_element_type=F32)


def growth(x):
    series = 1.0 + x * (1 / 2 + x * (1 / 6 + x * (1 / 24 + x * (1 / 120 + x * (
        1 / 720 + x * (1 / 5040 + x * (1 / 40320)))))))
    small = jnp.abs(x) < 0.5
    safe = jnp.where(small, 1.0, x)
    return jnp.where(small, series, (jnp.exp(x) - 1.0) / safe)


def iota(shape, axis):
    return lax.broadcasted_iota(jnp.int32, shape, axis)


def column(row):
    n = row.shape[1]
    eye = iota((n, n), 0) == iota((n, n), 1)
    return jnp.sum(jnp.where(eye, row, jnp.zeros_like(row)), axis=1, keepdims=True)


def biggest(u):
    used = iota((S, T), 0) < CODONS
    return jnp.max(jnp.where(used, u, 0.0), axis=0, keepdims=True)


def inverse(row):
    return pltpu.reciprocal(row, approx=True)


def held_integrals(basis2, lam2, lam_col, t):
    spread = (lam_col - lam2) * t
    return pack(basis2 * (t * jnp.exp(lam2 * t) * growth(spread)))


def local_children(parents, node):
    late, early = jnp.int32(0), jnp.int32(0)
    for c in range(LOC):
        hit = parents[c] == node
        early = jnp.where(hit, late, early)
        late = jnp.where(hit, c, late)
    return late, early


def slot_of(x, z, c):
    return c * (NX * NZ) + z * NX + x


def prepare(parents_h, lengths_h, top_lengths_h, top_parents_h, tips_h, vectors_h, inverse_h, lam_h, rates_h, freq_h,
            msg, w_top, w_loc, m_loc, y_loc, links, eig_w, inv_w, basis_out, lam_out, freq_out,
            parents, lengths, top_lengths, top_parents, tips, vectors, inverse_vectors, lam, rates, freq, x_int,
            in_sem, send_sem, recv_sem):
    me = lax.axis_index("leaf")
    site = lax.axis_index("site")
    core = lax.rem(me, 2)
    z = lax.rem(me // 2, NZ)
    x = me // (2 * NZ)

    loads = [pltpu.make_async_copy(src, dst, in_sem.at[i]) for i, (src, dst) in enumerate((
        (vectors_h, vectors), (inverse_h, inverse_vectors), (lam_h, lam), (lengths_h, lengths),
        (top_lengths_h, top_lengths), (tips_h, tips), (parents_h, parents), (rates_h, rates),
        (top_parents_h, top_parents), (freq_h, freq)))]
    for load in loads:
        load.start()

    def device(dx, dz, dc):
        nx, nz = lax.rem(x + dx + NX, NX), lax.rem(z + dz + NZ, NZ)
        nc = 1 - core if dc else core
        return ((nx * NZ + nz) * 2 + nc, site)

    x_peers = [(dx, 0, 0) for dx in (1, 2, 3)]
    partners = x_peers + [(0, dz, 0) for dz in range(1, NZ)] + [(0, 0, 1)]
    barrier = pltpu.get_barrier_semaphore()
    for partner in partners:
        pl.semaphore_signal(barrier, inc=1, device_id=device(*partner), device_id_type=MESH)

    for load in loads[:5]:
        load.wait()
    lam_row = lam[...]
    lam_col = column(lam_row)
    lam2 = double(lam_row)
    used = iota((S, S), 0) < CODONS
    right = jnp.where(used, vectors[...], 0.0)
    left = inverse_vectors[...]
    right2 = double(right)
    left_high, left_low = split(double(left))
    left_stack = jnp.concatenate([left_high, left_low, left_high, left_low], axis=0)
    r2, c2 = iota((S, T), 0), iota((S, T), 1)
    eye2 = jnp.where((r2 < CODONS) & ((r2 == c2) | (r2 + S == c2)), 1.0, 0.0)

    def branches(ts):
        scaled = []
        for t in ts:
            arg = lam2 * t
            scaled.append(pack(right2 * (arg * growth(arg))))
        result = jnp.dot(jnp.concatenate(scaled, axis=0), left_stack, preferred_element_type=F32)
        return [pack(eye2 + result[S * i:S * (i + 1)]) for i in range(len(ts))]

    for c, w in enumerate(branches([lengths[c] for c in range(LOC)] + [top_lengths[me]])):
        w_loc[c] = w

    loads[5].wait()
    loads[6].wait()
    for c in range(LEAVES):
        m_loc[c] = apply(w_loc[c], tips[c])
    factors = []
    for n in range(LEAVES, LOC + 1):
        a, b = local_children(parents, n)
        u = m_loc[a] * m_loc[b]
        r = inverse(biggest(u))
        factors.append(r)
        x_int[n - LEAVES] = u * r
        y = apply(w_loc[n], u) * r
        if n < LOC:
            m_loc[n] = y
        else:
            logs = -jnp.sum(jnp.log(jnp.concatenate(factors, axis=0)), axis=0, keepdims=True)
            msg[slot_of(x, z, core)] = jnp.where(iota((S, T), 0) == S - 1, logs, y)
    pl.semaphore_wait(barrier, len(partners))

    counter = [0]

    def block(bx, bz, bc):
        return msg.at[slot_of(bx, bz, bc)]

    def group(bz, bc):
        return msg.at[pl.ds(slot_of(0, bz, bc), NX)]

    started = []

    def send(piece, where, arriving):
        k = counter[0]
        counter[0] += 1
        copy = pltpu.make_async_remote_copy(src_ref=piece, dst_ref=piece, send_sem=send_sem.at[k],
                                            recv_sem=recv_sem.at[k], device_id=device(*where), device_id_type=MESH)
        copy.start()
        started.append(copy)
        incoming = pltpu.make_async_remote_copy(src_ref=arriving, dst_ref=arriving, send_sem=send_sem.at[k],
                                                recv_sem=recv_sem.at[k], device_id=device(*where), device_id_type=MESH)
        return incoming

    def at_z(dz):
        return lax.rem(z + dz + NZ, NZ)

    def at_x(dx):
        return lax.rem(x + dx + NX, NX)

    def along_z(dz):
        return send(block(x, z, core), (0, dz, 0), block(x, at_z(-dz), core))

    def along_x(dz):
        return [send(block(x, at_z(-dz), core), (dx, 0, 0), block(at_x(-dx), at_z(-dz), core)) for dx in (1, 3, 2)]

    def across(dz):
        return send(group(at_z(-dz), core), (0, 0, 1), group(at_z(-dz), 1 - core))

    def work(stage):
        if stage == 0:
            loads[7].wait()
            loads[8].wait()
            loads[9].wait()
            parent_col = column(top_parents[...])
            child = iota((TOP, T), 0)
            hit = parent_col == iota((TOP, T), 1)
            late = jnp.max(jnp.where(hit, child, 0), axis=0, keepdims=True)
            early = jnp.min(jnp.where(hit, child, TOP), axis=0, keepdims=True)
            pair = jnp.concatenate([late, early, jnp.zeros((6, T), jnp.int32)], axis=0)
            slots = (pair & 1) * (NX * NZ) + ((pair >> 1) & (NZ - 1)) * NX + (pair >> 4)
            pair = jnp.where(pair < GROUPS, slots, pair)
            lane = iota((8, T), 1)
            links[...] = jnp.where((lane >= GROUPS) & (lane <= ROOT), pair, 0)
            freq_out[...] = jnp.broadcast_to(column(freq[...]), (S, T))
            lam_out[...] = jnp.broadcast_to(lam2, (8, T))
            basis_out[...] = double(dot(dot(left, rates[...]), right))
            eig_w[...] = pack(right2)
            inv_w[...] = pack(double(left))
        elif stage <= 4:
            per = 4
            for c in range((stage - 1) * per, min(stage * per, LOC + 1)):
                t = lengths[c] if c < LOC else top_lengths[me]
                v = apply(inv_w[...], tips[c] if c < LEAVES else x_int[c - LEAVES])
                y_loc[c] = apply(eig_w[...], apply(held_integrals(basis_out[...], lam2, lam_col, t), v))
        else:
            lo, hi = ((0, 4), (4, 8))[stage - 5]

            def some(i, _):
                for j, w in enumerate(branches([top_lengths[jnp.minimum(GROUPS + i * 8 + j, TOP - 1)] for j in range(8)])):
                    w_top[i * 8 + j] = w
                return 0

            lax.fori_loop(lo, hi, some, 0)

    order = (1, -1, 2, -2, 3, -3, 4)
    from_x = {0: along_x(0)}
    from_z = {dz: along_z(dz) for dz in order}
    crossed = []

    def close(dz):
        for one in from_x[dz]:
            one.wait_recv()
        crossed.append(across(dz))

    work(0)
    for i, dz in enumerate(order):
        from_z[dz].wait_recv()
        from_x[dz] = along_x(dz)
        if i >= 1:
            close(((0,) + order)[i - 1])
        if i < 6:
            work(i + 1)
    for dz in order[-2:]:
        close(dz)
    for one in crossed:
        one.wait_recv()
    for one in started:
        one.wait_send()


COPIES = (NZ - 1) + 3 * NZ + NZ


def joining(top_parents_h, top_lengths_h, links, msg_in, w_top, freq, loglik, handed, info, msg,
            top_parents, top_lengths, path, factor, arrs, sem):
    del msg_in
    loads = [pltpu.make_async_copy(src, dst, sem.at[i]) for i, (src, dst) in enumerate((
        (top_parents_h, top_parents), (top_lengths_h, top_lengths)))]
    for load in loads:
        load.start()
    me = lax.axis_index("leaf")
    slot = slot_of(me // (2 * NZ), lax.rem(me // 2, NZ), lax.rem(me, 2))
    factor[...] = jnp.ones((72, T), F32)
    local_logs = msg[0, pl.ds(S - 1, 1)]
    for g in range(1, GROUPS):
        local_logs += msg[g, pl.ds(S - 1, 1)]

    def late(n):
        return links[0, n]

    def early(n):
        return links[1, n]

    def climb(n):
        done = []
        fits = True
        steps = jnp.int32(1)
        for j in range(WIN):
            k = jnp.minimum(n + j, T - 1) if j > 1 else n + j
            a, b = late(k), early(k)
            if j:
                fits = fits & (a < n)
                steps = steps + fits.astype(jnp.int32)
            u = msg[a] * msg[b]
            y = apply(w_top[jnp.minimum(k, ROOT) - GROUPS], u)
            r = inverse(biggest(u))
            done.append((y * r, r))
        for j, (y, r) in enumerate(done):
            msg[n + j] = y
            factor[pl.ds(n + j - GROUPS, 1)] = r
        return n + steps

    lax.while_loop(lambda n: n < ROOT, climb, jnp.int32(GROUPS))

    freq_col = freq[...]
    root_u = msg[late(ROOT)] * msg[early(ROOT)]
    likelihood = jnp.sum(freq_col * root_u, axis=0, keepdims=True)
    row = iota((72, T), 0)
    top_logs = -jnp.sum(jnp.log(jnp.where(row < TOP - GROUPS, factor[...], 1.0)), axis=0, keepdims=True)
    loglik[...] = (jnp.log(likelihood) + top_logs + local_logs) * (1.0 / (GROUPS * LEAVES))
    for load in loads:
        load.wait()

    def walk(state):
        c, depth, mine, at = state
        path[depth] = c
        p = top_parents[jnp.where(depth == 0, me, c)]
        found = (mine < 0) & (late(p) == c)
        return (p, depth + 1, jnp.where(found, p, mine), jnp.where(found, depth + 1, at))

    _, depth, mine, at = lax.while_loop(
        lambda state: state[0] != ROOT, walk, (slot, jnp.int32(0), jnp.int32(-1), jnp.int32(0)))
    counted = (mine >= 0) & (mine < ROOT)
    node = jnp.where(counted, mine, GROUPS)
    at = jnp.where(counted, at, 0)

    def step_down(i, o):
        k = depth - 1 - i
        c = path[k]
        p = top_parents[c]
        arriving = o * msg[late(p) + early(p) - c]
        arrs[k] = arriving
        return apply(w_top[c - GROUPS], arriving) * inverse(biggest(arriving))

    o = lax.fori_loop(0, depth - 1, step_down, jnp.ones((S, T), F32))
    p = top_parents[me]
    leaf_arriving = o * msg[late(p) + early(p) - slot]
    arrs[0] = leaf_arriving
    handed[0] = leaf_arriving
    handed[1] = msg[slot]
    handed[2] = arrs[at]
    handed[3] = msg[node]
    handed[4] = msg[late(node)] * msg[early(node)] * factor[pl.ds(node - GROUPS, 1)]
    row = iota((8, T), 0)
    info[...] = jnp.where(row == 0, top_lengths[node], jnp.where(counted, node, -1).astype(F32))


PHASES = ("y", "c", "x", "z")


def tail(parents_h, weights_h, handed, info, w_loc, m_loc, y_loc, eig_w, inv_w, basis, lam, freq, local_out, top_out,
         parents, weights, o_loc, rows, *rest):
    bufs, parts = rest[:len(PHASES)], rest[len(PHASES):2 * len(PHASES)]
    in_sem, send_sem, recv_sem = rest[2 * len(PHASES):]
    loads = [pltpu.make_async_copy(parents_h, parents, in_sem.at[0]), pltpu.make_async_copy(weights_h, weights, in_sem.at[1])]
    for load in loads:
        load.start()
    me = lax.axis_index("leaf")
    sizes = {"x": NX, "z": NZ, "c": 2, "y": lax.axis_size("site")}
    here = {"x": me // (2 * NZ), "z": lax.rem(me // 2, NZ), "c": lax.rem(me, 2), "y": lax.axis_index("site")}

    def shifted(offset):
        return {a: (lax.rem(here[a] + offset.get(a, 0) + sizes[a], sizes[a])) for a in here}

    def device(offset):
        at = shifted(offset)
        return ((at["x"] * NZ + at["z"]) * 2 + at["c"], at["y"])

    def place(axes, at):
        index = 0
        for a in axes:
            index = index * sizes[a] + at[a]
        return index

    offsets = [phase_offsets(axes, sizes) for axes in PHASES]
    barrier = pltpu.get_barrier_semaphore()
    for some in offsets:
        for offset in some:
            pl.semaphore_signal(barrier, inc=1, device_id=device(offset), device_id_type=MESH)

    freq_col = freq[...]

    def ratio(row, arriving, message, y):
        weighted = freq_col * arriving
        rows[0, pl.ds(row, 1)] = jnp.sum(weighted * y, axis=0, keepdims=True)
        rows[1, pl.ds(row, 1)] = jnp.sum(weighted * message, axis=0, keepdims=True)

    rows[...] = jnp.ones((2, 24, T), F32)
    lam2 = lam[0:1]
    o_loc[LOC - LEAVES] = apply(w_loc[LOC], handed[0]) * inverse(biggest(handed[0]))
    ratio(16, handed[0], handed[1], y_loc[LOC])
    held = held_integrals(basis[...], lam2, column(lam2[:, :S]), info[0:1, 0:1])
    ratio(17, handed[2], handed[3], apply(eig_w[...], apply(held, apply(inv_w[...], handed[4]))))
    for load in loads:
        load.wait()
    for c in range(LOC - 1, -1, -1):
        p = jnp.clip(parents[c], LEAVES, LOC)
        sibling = jnp.int32(0)
        for other in range(LOC):
            if other != c:
                sibling = jnp.where(parents[other] == p, other, sibling)
        arriving = o_loc[p - LEAVES] * m_loc[sibling]
        if c >= LEAVES:
            o_loc[c - LEAVES] = apply(w_loc[c], arriving) * inverse(biggest(arriving))
        ratio(c, arriving, m_loc[c], y_loc[c])
    weight = weights[...].astype(F32)
    expected = jnp.where(iota((24, T), 0) == LOC, weight, weight * rows[0] / rows[1])
    sums = lax.dot_general(jnp.ones((8, T), F32), expected, (((1,), (1,)), ((), ())),
                           precision=PRECISE, preferred_element_type=F32)
    lane = iota((1, T), 1)
    node = info[1:2]
    top_row = jnp.where(lane == me, sums[0:1, 16:17], 0.0) + jnp.where(lane.astype(F32) == node, sums[0:1, 17:18], 0.0)
    parts[0][...] = jnp.zeros((8, T), F32)
    parts[0][pl.ds(0, 1), pl.ds(0, 24)] = sums[0:1]
    parts[0][pl.ds(1, 1)] = top_row
    pl.semaphore_wait(barrier, sum(map(len, offsets)))

    k = 0
    copies = []
    for i, (axes, some) in enumerate(zip(PHASES, offsets)):
        buf, part = bufs[i], parts[i]
        mine = place(axes, here)
        buf[mine] = part[...]
        arrivals = []
        for offset in some:
            copy = pltpu.make_async_remote_copy(src_ref=part, dst_ref=buf.at[mine], send_sem=send_sem.at[k],
                                                recv_sem=recv_sem.at[k], device_id=device(offset), device_id_type=MESH)
            copy.start()
            copies.append(copy)
            there = buf.at[place(axes, shifted({a: -n for a, n in offset.items()}))]
            arrivals.append(pltpu.make_async_remote_copy(
                src_ref=there, dst_ref=there, send_sem=send_sem.at[k], recv_sem=recv_sem.at[k],
                device_id=device(offset), device_id_type=MESH))
            k += 1
        for arrival in arrivals:
            arrival.wait_recv()
        total = jnp.sum(buf[...], axis=0)
        if i == 0:
            weight_total = total[0:1, LOC:LOC + 1]
            local_out[...] = (total[0:1] / weight_total)[:, :LOC]
        if i + 1 < len(PHASES):
            parts[i + 1][...] = total
    top_out[...] = (total[1:2] / weight_total)[:, :TOP]
    for copy in copies:
        copy.wait_send()


def phase_offsets(axes, sizes):
    found = [{}]
    for a in axes:
        found = [{**one, a: n} for one in found for n in range(sizes[a])]
    return [one for one in found if any(one.values())]


def on_device(tips, parents, branch_lengths, top_parents, top_lengths, weights, eig_vectors,
              eig_inverse, eig_values, labeled_rates, root_freq):
    hbm = pl.BlockSpec(memory_space=pltpu.HBM)
    stay = functools.partial(pltpu.with_memory_space_constraint, memory_space=pltpu.HBM)
    smem = pl.BlockSpec(memory_space=pltpu.SMEM)
    vmem = pl.BlockSpec(memory_space=pltpu.VMEM)
    shape = jax.ShapeDtypeStruct
    msg, *made = pl.pallas_call(
        prepare,
        out_shape=(
            shape((ROOT + 1 + WIN, S, T), F32),
            shape((GROUPS, S, 256), BF16),
            shape((LOC + 1, S, 256), BF16),
            shape((LOC, S, T), F32),
            shape((LOC + 1, S, T), F32),
            shape((8, T), jnp.int32),
            shape((S, 256), BF16),
            shape((S, 256), BF16),
            shape((S, T), F32),
            shape((8, T), F32),
            shape((S, T), F32),
        ),
        in_specs=[hbm] * 10,
        out_specs=(vmem,) * 11,
        scratch_shapes=[
            pltpu.SMEM((LOC,), jnp.int32),
            pltpu.SMEM((LOC,), F32),
            pltpu.SMEM((TOP,), F32),
            pltpu.VMEM((1, TOP), jnp.int32),
            pltpu.VMEM((LEAVES, S, T), F32),
            pltpu.VMEM((S, S), F32),
            pltpu.VMEM((S, S), F32),
            pltpu.VMEM((1, S), F32),
            pltpu.VMEM((S, S), F32),
            pltpu.VMEM((1, S), F32),
            pltpu.VMEM((8, S, T), F32),
            pltpu.SemaphoreType.DMA((10,)),
            pltpu.SemaphoreType.DMA((COPIES,)),
            pltpu.SemaphoreType.DMA((COPIES,)),
        ],
        compiler_params=pltpu.CompilerParams(vmem_limit_bytes=40 << 20, collective_id=0, has_side_effects=True),
        name="prepare",
    )(*map(stay, (parents, branch_lengths, top_lengths, top_parents.reshape(1, TOP), tips, eig_vectors, eig_inverse,
                   eig_values.reshape(1, S), labeled_rates, root_freq.reshape(1, S))))
    w_top, w_loc, m_loc, y_loc, links, eig_w, inv_w, basis, lam, freq = made
    loglik, handed, info, _ = pl.pallas_call(
        joining,
        out_shape=(shape((1, T), F32), shape((5, S, T), F32), shape((8, T), F32), shape(msg.shape, F32)),
        in_specs=[hbm] * 2 + [smem] + [vmem] * 3,
        out_specs=(vmem,) * 4,
        input_output_aliases={3: 3},
        scratch_shapes=[
            pltpu.SMEM((TOP,), jnp.int32),
            pltpu.SMEM((TOP,), F32),
            pltpu.SMEM((64,), jnp.int32),
            pltpu.VMEM((72, T), F32),
            pltpu.VMEM((GROUPS, S, T), F32),
            pltpu.SemaphoreType.DMA((2,)),
        ],
        compiler_params=pltpu.CompilerParams(vmem_limit_bytes=24 << 20),
        name="joining",
    )(*map(stay, (top_parents, top_lengths)), links, msg, w_top, freq)
    sizes = {"x": NX, "z": NZ, "c": 2, "y": lax.axis_size("site")}
    offsets = [phase_offsets(axes, sizes) for axes in PHASES]
    count = sum(map(len, offsets))
    local, top = pl.pallas_call(
        tail,
        out_shape=(shape((1, LOC), F32), shape((1, TOP), F32)),
        in_specs=[hbm] * 2 + [vmem] * 10,
        out_specs=(vmem, vmem),
        scratch_shapes=[
            pltpu.SMEM((LOC,), jnp.int32),
            pltpu.VMEM((1, T), jnp.int32),
            pltpu.VMEM((8, S, T), F32),
            pltpu.VMEM((2, 24, T), F32),
        ] + [pltpu.VMEM((len(some) + 1, 8, T), F32) for some in offsets] + [pltpu.VMEM((8, T), F32) for _ in offsets] + [
            pltpu.SemaphoreType.DMA((2,)),
            pltpu.SemaphoreType.DMA((count,)),
            pltpu.SemaphoreType.DMA((count,)),
        ],
        compiler_params=pltpu.CompilerParams(vmem_limit_bytes=24 << 20, collective_id=1, has_side_effects=True),
        name="tail",
    )(*map(stay, (parents, weights.reshape(1, T))), handed, info, w_loc, m_loc, y_loc, eig_w, inv_w, basis, lam, freq)
    return local.reshape(LOC), top.reshape(TOP), loglik.reshape(T)


def solution(mesh):
    placed = (P("leaf", None, "site"), P("leaf"), P("leaf"), P(), P(), P("site"), P(), P(), P(), P(), P())
    return jax.shard_map(
        on_device,
        mesh=mesh,
        in_specs=placed,
        out_specs=(P("leaf"), P(), P("site")),
        check_vma=False,
    )
```

```python
import functools

import jax
import jax.numpy as jnp
from jax import lax
from jax.experimental import pallas as pl
from jax.experimental.pallas import tpu as pltpu
from jax.sharding import PartitionSpec as P

CODONS = 61
S = 64
T = 128
LEAVES = 8
LOC = 14
GROUPS = 64
TOP = 126
ROOT = 126
WIN = 6
ACROSS = 16
F32 = jnp.float32
BF16 = jnp.bfloat16
PRECISE = lax.Precision.HIGHEST
NX, NZ = 4, 8
MESH = pl.DeviceIdType.MESH


def split(u):
    high = u.astype(BF16)
    low = (u - high.astype(F32)).astype(BF16)
    return high, low


def apply(w, u):
    high, low = split(u)
    return jnp.dot(w, jnp.concatenate([high, low, high, low], axis=0), preferred_element_type=F32)


def pack(doubled):
    high, low = split(doubled)
    return jnp.concatenate([high, low], axis=1)


def double(a):
    return jnp.concatenate([a, a], axis=1)


def dot(a, b):
    return jnp.dot(a, b, precision=PRECISE, preferred_element_type=F32)


def growth(x):
    series = 1.0 + x * (1 / 2 + x * (1 / 6 + x * (1 / 24 + x * (1 / 120 + x * (
        1 / 720 + x * (1 / 5040 + x * (1 / 40320)))))))
    small = jnp.abs(x) < 0.5
    safe = jnp.where(small, 1.0, x)
    return jnp.where(small, series, (jnp.exp(x) - 1.0) / safe)


def iota(shape, axis):
    return lax.broadcasted_iota(jnp.int32, shape, axis)


def column(row):
    n = row.shape[1]
    eye = iota((n, n), 0) == iota((n, n), 1)
    return jnp.sum(jnp.where(eye, row, jnp.zeros_like(row)), axis=1, keepdims=True)


def biggest(u):
    used = iota((S, T), 0) < CODONS
    return jnp.max(jnp.where(used, u, 0.0), axis=0, keepdims=True)


def inverse(row):
    return pltpu.reciprocal(row, approx=True)


def held_integrals(basis2, lam2, lam_col, t):
    spread = (lam_col - lam2) * t
    return pack(basis2 * (t * jnp.exp(lam2 * t) * growth(spread)))


def local_children(parents, node):
    late, early = jnp.int32(0), jnp.int32(0)
    for c in range(LOC):
        hit = parents[c] == node
        early = jnp.where(hit, late, early)
        late = jnp.where(hit, c, late)
    return late, early


def slot_of(x, z, c):
    return c * (NX * NZ) + z * NX + x


def prepare(parents_h, lengths_h, top_lengths_h, top_parents_h, tips_h, vectors_h, inverse_h, lam_h, rates_h, freq_h,
            msg, w_top, w_loc, m_loc, y_loc, links, eig_w, inv_w, basis_out, lam_out, freq_out,
            parents, lengths, top_lengths, top_parents, tips, vectors, inverse_vectors, lam, rates, freq, x_int,
            in_sem, send_sem, recv_sem):
    me = lax.axis_index("leaf")
    site = lax.axis_index("site")
    core = lax.rem(me, 2)
    z = lax.rem(me // 2, NZ)
    x = me // (2 * NZ)

    loads = [pltpu.make_async_copy(src, dst, in_sem.at[i]) for i, (src, dst) in enumerate((
        (vectors_h, vectors), (inverse_h, inverse_vectors), (lam_h, lam), (lengths_h, lengths),
        (top_lengths_h, top_lengths), (tips_h, tips), (parents_h, parents), (rates_h, rates),
        (top_parents_h, top_parents), (freq_h, freq)))]
    for load in loads:
        load.start()

    def device(dx, dz, dc):
        nx, nz = lax.rem(x + dx + NX, NX), lax.rem(z + dz + NZ, NZ)
        nc = 1 - core if dc else core
        return ((nx * NZ + nz) * 2 + nc, site)

    x_peers = [(dx, 0, 0) for dx in (1, 2, 3)]
    partners = x_peers + [(0, dz, 0) for dz in range(1, NZ)] + [(0, 0, 1)]
    barrier = pltpu.get_barrier_semaphore()
    for partner in partners:
        pl.semaphore_signal(barrier, inc=1, device_id=device(*partner), device_id_type=MESH)

    for load in loads[:5]:
        load.wait()
    lam_row = lam[...]
    lam_col = column(lam_row)
    lam2 = double(lam_row)
    used = iota((S, S), 0) < CODONS
    right = jnp.where(used, vectors[...], 0.0)
    left = inverse_vectors[...]
    right2 = double(right)
    left_high, left_low = split(double(left))
    left_stack = jnp.concatenate([left_high, left_low, left_high, left_low], axis=0)
    r2, c2 = iota((S, T), 0), iota((S, T), 1)
    eye2 = jnp.where((r2 < CODONS) & ((r2 == c2) | (r2 + S == c2)), 1.0, 0.0)

    def branches(ts):
        scaled = []
        for t in ts:
            arg = lam2 * t
            scaled.append(pack(right2 * (arg * growth(arg))))
        result = jnp.dot(jnp.concatenate(scaled, axis=0), left_stack, preferred_element_type=F32)
        return [pack(eye2 + result[S * i:S * (i + 1)]) for i in range(len(ts))]

    for c, w in enumerate(branches([lengths[c] for c in range(LOC)] + [top_lengths[me]])):
        w_loc[c] = w

    loads[5].wait()
    loads[6].wait()
    for c in range(LEAVES):
        m_loc[c] = apply(w_loc[c], tips[c])
    factors = []
    for n in range(LEAVES, LOC + 1):
        a, b = local_children(parents, n)
        u = m_loc[a] * m_loc[b]
        r = inverse(biggest(u))
        factors.append(r)
        x_int[n - LEAVES] = u * r
        y = apply(w_loc[n], u) * r
        if n < LOC:
            m_loc[n] = y
        else:
            logs = -jnp.sum(jnp.log(jnp.concatenate(factors, axis=0)), axis=0, keepdims=True)
            msg[slot_of(x, z, core)] = jnp.where(iota((S, T), 0) == S - 1, logs, y)
    pl.semaphore_wait(barrier, len(partners))

    counter = [0]

    main, rest = pl.ds(0, S - ACROSS), pl.ds(S - ACROSS, ACROSS)

    def block(bx, bz, bc, rows):
        return msg.at[slot_of(bx, bz, bc), rows]

    def group(bz, bc, rows):
        return msg.at[pl.ds(slot_of(0, bz, bc), NX), rows]

    started = []

    def send(piece, where, arriving):
        k = counter[0]
        counter[0] += 1
        copy = pltpu.make_async_remote_copy(src_ref=piece, dst_ref=piece, send_sem=send_sem.at[k],
                                            recv_sem=recv_sem.at[k], device_id=device(*where), device_id_type=MESH)
        copy.start()
        started.append(copy)
        incoming = pltpu.make_async_remote_copy(src_ref=arriving, dst_ref=arriving, send_sem=send_sem.at[k],
                                                recv_sem=recv_sem.at[k], device_id=device(*where), device_id_type=MESH)
        return incoming

    def at_z(dz):
        return lax.rem(z + dz + NZ, NZ)

    def at_x(dx):
        return lax.rem(x + dx + NX, NX)

    def along_z(dz):
        return send(block(x, z, core, main), (0, dz, 0), block(x, at_z(-dz), core, main))

    def along_x(dz, rows):
        return [send(block(x, at_z(-dz), core, rows), (dx, 0, 0), block(at_x(-dx), at_z(-dz), core, rows))
                for dx in (1, 3, 2)]

    def group_z(dz):
        return send(group(z, core, rest), (0, dz, 0), group(at_z(-dz), core, rest))

    def across(dz, rows):
        return send(group(at_z(-dz), core, rows), (0, 0, 1), group(at_z(-dz), 1 - core, rows))

    def shared():
        loads[7].wait()
        loads[8].wait()
        loads[9].wait()
        parent_col = column(top_parents[...])
        child = iota((TOP, T), 0)
        hit = parent_col == iota((TOP, T), 1)
        late = jnp.max(jnp.where(hit, child, 0), axis=0, keepdims=True)
        early = jnp.min(jnp.where(hit, child, TOP), axis=0, keepdims=True)
        pair = jnp.concatenate([late, early, jnp.zeros((6, T), jnp.int32)], axis=0)
        slots = (pair & 1) * (NX * NZ) + ((pair >> 1) & (NZ - 1)) * NX + (pair >> 4)
        pair = jnp.where(pair < GROUPS, slots, pair)
        lane = iota((8, T), 1)
        links[...] = jnp.where((lane >= GROUPS) & (lane <= ROOT), pair, 0)
        freq_out[...] = jnp.broadcast_to(column(freq[...]), (S, T))
        lam_out[...] = jnp.broadcast_to(lam2, (8, T))
        basis_out[...] = double(dot(dot(left, rates[...]), right))
        eig_w[...] = pack(right2)
        inv_w[...] = pack(double(left))

    def products(lo, hi):
        for c in range(lo, hi):
            t = lengths[c] if c < LOC else top_lengths[me]
            v = apply(inv_w[...], tips[c] if c < LEAVES else x_int[c - LEAVES])
            y_loc[c] = apply(eig_w[...], apply(held_integrals(basis_out[...], lam2, lam_col, t), v))

    def matrices(lo, hi):
        def some(i, _):
            ts = [top_lengths[jnp.minimum(GROUPS + i * 8 + j, TOP - 1)] for j in range(8)]
            for j, w in enumerate(branches(ts)):
                w_top[i * 8 + j] = w
            return 0

        lax.fori_loop(lo, hi, some, 0)

    order = (1, -1, 2, -2, 3, -3, 4)
    turns = (0,) + order
    first = along_x(0, rest)
    from_z = {dz: along_z(dz) for dz in order[:2]}
    from_x = {0: along_x(0, main)}
    from_z.update({dz: along_z(dz) for dz in order[2:]})
    crossed = []
    closed = [0]

    def close():
        dz = turns[closed[0]]
        closed[0] += 1
        for one in from_x[dz]:
            one.wait_recv()
        crossed.append(across(dz, main))

    shared()
    for i, dz in enumerate(order):
        from_z[dz].wait_recv()
        from_x[dz] = along_x(dz, main)
        if i == 0:
            for one in first:
                one.wait_recv()
            groups = {d: group_z(d) for d in order}
            crossed.append(across(0, rest))
        if i >= 5:
            close()
        if i in (1, 3, 5):
            matrices(i - 1, i + 1)
    products(0, 5)
    for i, dz in enumerate(order):
        groups[dz].wait_recv()
        crossed.append(across(dz, rest))
        if closed[0] < len(turns):
            close()
        if i == 1:
            products(5, 10)
        if i == 3:
            products(10, 15)
        if i == 5:
            matrices(6, 8)
    while closed[0] < len(turns):
        close()
    for one in crossed:
        one.wait_recv()
    for one in started:
        one.wait_send()


COPIES = 3 * (NZ + 1) + 2 * (NZ - 1) + 2 * NZ


def joining(top_parents_h, top_lengths_h, links, msg_in, w_top, freq, loglik, handed, info, msg,
            top_parents, top_lengths, path, factor, arrs, sem):
    del msg_in
    loads = [pltpu.make_async_copy(src, dst, sem.at[i]) for i, (src, dst) in enumerate((
        (top_parents_h, top_parents), (top_lengths_h, top_lengths)))]
    for load in loads:
        load.start()
    me = lax.axis_index("leaf")
    slot = slot_of(me // (2 * NZ), lax.rem(me // 2, NZ), lax.rem(me, 2))
    factor[...] = jnp.ones((72, T), F32)
    local_logs = msg[0, pl.ds(S - 1, 1)]
    for g in range(1, GROUPS):
        local_logs += msg[g, pl.ds(S - 1, 1)]

    def late(n):
        return links[0, n]

    def early(n):
        return links[1, n]

    def climb(n):
        done = []
        fits = True
        steps = jnp.int32(1)
        for j in range(WIN):
            k = jnp.minimum(n + j, T - 1) if j > 1 else n + j
            a, b = late(k), early(k)
            if j:
                fits = fits & (a < n)
                steps = steps + fits.astype(jnp.int32)
            u = msg[a] * msg[b]
            y = apply(w_top[jnp.minimum(k, ROOT) - GROUPS], u)
            r = inverse(biggest(u))
            done.append((y * r, r))
        for j, (y, r) in enumerate(done):
            msg[n + j] = y
            factor[pl.ds(n + j - GROUPS, 1)] = r
        return n + steps

    lax.while_loop(lambda n: n < ROOT, climb, jnp.int32(GROUPS))

    freq_col = freq[...]
    root_u = msg[late(ROOT)] * msg[early(ROOT)]
    likelihood = jnp.sum(freq_col * root_u, axis=0, keepdims=True)
    row = iota((72, T), 0)
    top_logs = -jnp.sum(jnp.log(jnp.where(row < TOP - GROUPS, factor[...], 1.0)), axis=0, keepdims=True)
    loglik[...] = (jnp.log(likelihood) + top_logs + local_logs) * (1.0 / (GROUPS * LEAVES))
    for load in loads:
        load.wait()

    def walk(state):
        c, depth, mine, at = state
        path[depth] = c
        p = top_parents[jnp.where(depth == 0, me, c)]
        found = (mine < 0) & (late(p) == c)
        return (p, depth + 1, jnp.where(found, p, mine), jnp.where(found, depth + 1, at))

    _, depth, mine, at = lax.while_loop(
        lambda state: state[0] != ROOT, walk, (slot, jnp.int32(0), jnp.int32(-1), jnp.int32(0)))
    counted = (mine >= 0) & (mine < ROOT)
    node = jnp.where(counted, mine, GROUPS)
    at = jnp.where(counted, at, 0)

    def step_down(i, o):
        k = depth - 1 - i
        c = path[k]
        p = top_parents[c]
        arriving = o * msg[late(p) + early(p) - c]
        arrs[k] = arriving
        return apply(w_top[c - GROUPS], arriving) * inverse(biggest(arriving))

    o = lax.fori_loop(0, depth - 1, step_down, jnp.ones((S, T), F32))
    p = top_parents[me]
    leaf_arriving = o * msg[late(p) + early(p) - slot]
    arrs[0] = leaf_arriving
    handed[0] = leaf_arriving
    handed[1] = msg[slot]
    handed[2] = arrs[at]
    handed[3] = msg[node]
    handed[4] = msg[late(node)] * msg[early(node)] * factor[pl.ds(node - GROUPS, 1)]
    row = iota((8, T), 0)
    info[...] = jnp.where(row == 0, top_lengths[node], jnp.where(counted, node, -1).astype(F32))


PHASES = ("yc", "x", "z")


def tail(parents_h, weights_h, handed, info, w_loc, m_loc, y_loc, eig_w, inv_w, basis, lam, freq, local_out, top_out,
         parents, weights, o_loc, rows, *rest):
    bufs, parts = rest[:len(PHASES)], rest[len(PHASES):2 * len(PHASES)]
    in_sem, send_sem, recv_sem = rest[2 * len(PHASES):]
    loads = [pltpu.make_async_copy(parents_h, parents, in_sem.at[0]), pltpu.make_async_copy(weights_h, weights, in_sem.at[1])]
    for load in loads:
        load.start()
    me = lax.axis_index("leaf")
    sizes = {"x": NX, "z": NZ, "c": 2, "y": lax.axis_size("site")}
    here = {"x": me // (2 * NZ), "z": lax.rem(me // 2, NZ), "c": lax.rem(me, 2), "y": lax.axis_index("site")}

    def shifted(offset):
        return {a: (lax.rem(here[a] + offset.get(a, 0) + sizes[a], sizes[a])) for a in here}

    def device(offset):
        at = shifted(offset)
        return ((at["x"] * NZ + at["z"]) * 2 + at["c"], at["y"])

    def place(axes, at):
        index = 0
        for a in axes:
            index = index * sizes[a] + at[a]
        return index

    offsets = [phase_offsets(axes, sizes) for axes in PHASES]
    barrier = pltpu.get_barrier_semaphore()
    for some in offsets:
        for offset in some:
            pl.semaphore_signal(barrier, inc=1, device_id=device(offset), device_id_type=MESH)

    freq_col = freq[...]

    def ratio(row, arriving, message, y):
        weighted = freq_col * arriving
        rows[0, pl.ds(row, 1)] = jnp.sum(weighted * y, axis=0, keepdims=True)
        rows[1, pl.ds(row, 1)] = jnp.sum(weighted * message, axis=0, keepdims=True)

    rows[...] = jnp.ones((2, 24, T), F32)
    lam2 = lam[0:1]
    o_loc[LOC - LEAVES] = apply(w_loc[LOC], handed[0]) * inverse(biggest(handed[0]))
    ratio(16, handed[0], handed[1], y_loc[LOC])
    held = held_integrals(basis[...], lam2, column(lam2[:, :S]), info[0:1, 0:1])
    ratio(17, handed[2], handed[3], apply(eig_w[...], apply(held, apply(inv_w[...], handed[4]))))
    for load in loads:
        load.wait()
    for c in range(LOC - 1, -1, -1):
        p = jnp.clip(parents[c], LEAVES, LOC)
        sibling = jnp.int32(0)
        for other in range(LOC):
            if other != c:
                sibling = jnp.where(parents[other] == p, other, sibling)
        arriving = o_loc[p - LEAVES] * m_loc[sibling]
        if c >= LEAVES:
            o_loc[c - LEAVES] = apply(w_loc[c], arriving) * inverse(biggest(arriving))
        ratio(c, arriving, m_loc[c], y_loc[c])
    weight = weights[...].astype(F32)
    expected = jnp.where(iota((24, T), 0) == LOC, weight, weight * rows[0] / rows[1])
    expected = jnp.concatenate([expected, jnp.zeros((T - 24, T), F32)], axis=0)
    sums = lax.dot_general(jnp.ones((8, T), F32), expected, (((1,), (1,)), ((), ())),
                           precision=PRECISE, preferred_element_type=F32)
    lane = iota((1, T), 1)
    node = info[1:2]
    top_row = jnp.where(lane == me, sums[0:1, 16:17], 0.0) + jnp.where(lane.astype(F32) == node, sums[0:1, 17:18], 0.0)
    parts[0][...] = jnp.concatenate([sums[0:1], top_row], axis=0)
    pl.semaphore_wait(barrier, sum(map(len, offsets)))

    k = 0
    copies = []
    for i, (axes, some) in enumerate(zip(PHASES, offsets)):
        buf, part = bufs[i], parts[i]
        mine = place(axes, here)
        buf[mine] = part[...]
        arrivals = []
        for offset in some:
            copy = pltpu.make_async_remote_copy(src_ref=part, dst_ref=buf.at[mine], send_sem=send_sem.at[k],
                                                recv_sem=recv_sem.at[k], device_id=device(offset), device_id_type=MESH)
            copy.start()
            copies.append(copy)
            there = buf.at[place(axes, shifted({a: -n for a, n in offset.items()}))]
            arrivals.append(pltpu.make_async_remote_copy(
                src_ref=there, dst_ref=there, send_sem=send_sem.at[k], recv_sem=recv_sem.at[k],
                device_id=device(offset), device_id_type=MESH))
            k += 1
        for arrival in arrivals:
            arrival.wait_recv()
        if i == 0:
            local = buf[here["c"], 0:1]
            total = buf[0, 1:2] + buf[1, 1:2]
            for n in range(1, sizes["y"]):
                local = local + buf[2 * n + here["c"], 0:1]
                total = total + (buf[2 * n, 1:2] + buf[2 * n + 1, 1:2])
            weight_total = local[:, LOC:LOC + 1]
            local_out[...] = (local / weight_total)[:, :LOC]
        else:
            total = buf[0]
            for n in range(1, len(some) + 1):
                total = total + buf[n]
        if i + 1 < len(PHASES):
            parts[i + 1][...] = total
    top_out[...] = (total / weight_total)[:, :TOP]
    for copy in copies:
        copy.wait_send()


def phase_offsets(axes, sizes):
    found = [{}]
    for a in axes:
        found = [{**one, a: n} for one in found for n in range(sizes[a])]
    return [one for one in found if any(one.values())]


def on_device(tips, parents, branch_lengths, top_parents, top_lengths, weights, eig_vectors,
              eig_inverse, eig_values, labeled_rates, root_freq):
    hbm = pl.BlockSpec(memory_space=pltpu.HBM)
    stay = functools.partial(pltpu.with_memory_space_constraint, memory_space=pltpu.HBM)
    smem = pl.BlockSpec(memory_space=pltpu.SMEM)
    vmem = pl.BlockSpec(memory_space=pltpu.VMEM)
    shape = jax.ShapeDtypeStruct
    msg, *made = pl.pallas_call(
        prepare,
        out_shape=(
            shape((ROOT + 1 + WIN, S, T), F32),
            shape((GROUPS, S, 256), BF16),
            shape((LOC + 1, S, 256), BF16),
            shape((LOC, S, T), F32),
            shape((LOC + 1, S, T), F32),
            shape((8, T), jnp.int32),
            shape((S, 256), BF16),
            shape((S, 256), BF16),
            shape((S, T), F32),
            shape((8, T), F32),
            shape((S, T), F32),
        ),
        in_specs=[hbm] * 10,
        out_specs=(vmem,) * 11,
        scratch_shapes=[
            pltpu.SMEM((LOC,), jnp.int32),
            pltpu.SMEM((LOC,), F32),
            pltpu.SMEM((TOP,), F32),
            pltpu.VMEM((1, TOP), jnp.int32),
            pltpu.VMEM((LEAVES, S, T), F32),
            pltpu.VMEM((S, S), F32),
            pltpu.VMEM((S, S), F32),
            pltpu.VMEM((1, S), F32),
            pltpu.VMEM((S, S), F32),
            pltpu.VMEM((1, S), F32),
            pltpu.VMEM((8, S, T), F32),
            pltpu.SemaphoreType.DMA((10,)),
            pltpu.SemaphoreType.DMA((COPIES,)),
            pltpu.SemaphoreType.DMA((COPIES,)),
        ],
        compiler_params=pltpu.CompilerParams(vmem_limit_bytes=40 << 20, collective_id=0, has_side_effects=True),
        name="prepare",
    )(*map(stay, (parents, branch_lengths, top_lengths, top_parents.reshape(1, TOP), tips, eig_vectors, eig_inverse,
                   eig_values.reshape(1, S), labeled_rates, root_freq.reshape(1, S))))
    w_top, w_loc, m_loc, y_loc, links, eig_w, inv_w, basis, lam, freq = made
    loglik, handed, info, _ = pl.pallas_call(
        joining,
        out_shape=(shape((1, T), F32), shape((5, S, T), F32), shape((8, T), F32), shape(msg.shape, F32)),
        in_specs=[hbm] * 2 + [smem] + [vmem] * 3,
        out_specs=(vmem,) * 4,
        input_output_aliases={3: 3},
        scratch_shapes=[
            pltpu.SMEM((TOP,), jnp.int32),
            pltpu.SMEM((TOP,), F32),
            pltpu.SMEM((64,), jnp.int32),
            pltpu.VMEM((72, T), F32),
            pltpu.VMEM((GROUPS, S, T), F32),
            pltpu.SemaphoreType.DMA((2,)),
        ],
        compiler_params=pltpu.CompilerParams(vmem_limit_bytes=24 << 20),
        name="joining",
    )(*map(stay, (top_parents, top_lengths)), links, msg, w_top, freq)
    sizes = {"x": NX, "z": NZ, "c": 2, "y": lax.axis_size("site")}
    offsets = [phase_offsets(axes, sizes) for axes in PHASES]
    count = sum(map(len, offsets))
    local, top = pl.pallas_call(
        tail,
        out_shape=(shape((1, LOC), F32), shape((1, TOP), F32)),
        in_specs=[hbm] * 2 + [vmem] * 10,
        out_specs=(vmem, vmem),
        scratch_shapes=[
            pltpu.SMEM((LOC,), jnp.int32),
            pltpu.VMEM((1, T), jnp.int32),
            pltpu.VMEM((8, S, T), F32),
            pltpu.VMEM((2, 24, T), F32),
        ] + [pltpu.VMEM((len(some) + 1, 1 if i else 2, T), F32) for i, some in enumerate(offsets)] + [
            pltpu.VMEM((1 if i else 2, T), F32) for i in range(len(offsets))] + [
            pltpu.SemaphoreType.DMA((2,)),
            pltpu.SemaphoreType.DMA((count,)),
            pltpu.SemaphoreType.DMA((count,)),
        ],
        compiler_params=pltpu.CompilerParams(vmem_limit_bytes=24 << 20, collective_id=1, has_side_effects=True),
        name="tail",
    )(*map(stay, (parents, weights.reshape(1, T))), handed, info, w_loc, m_loc, y_loc, eig_w, inv_w, basis, lam, freq)
    return local.reshape(LOC), top.reshape(TOP), loglik.reshape(T)


def solution(mesh):
    placed = (P("leaf", None, "site"), P("leaf"), P("leaf"), P(), P(), P("site"), P(), P(), P(), P(), P())
    return jax.shard_map(
        on_device,
        mesh=mesh,
        in_specs=placed,
        out_specs=(P("leaf"), P(), P("site")),
        check_vma=False,
    )
```

```python
import functools

import jax
import jax.numpy as jnp
from jax import lax
from jax.experimental import pallas as pl
from jax.experimental.pallas import tpu as pltpu
from jax.sharding import PartitionSpec as P

CODONS = 61
S = 64
T = 128
LEAVES = 8
LOC = 14
GROUPS = 64
TOP = 126
ROOT = 126
WIN = 6
ACROSS = 16
F32 = jnp.float32
BF16 = jnp.bfloat16
PRECISE = lax.Precision.HIGHEST
NX, NZ = 4, 8
MESH = pl.DeviceIdType.MESH


def split(u):
    high = u.astype(BF16)
    low = (u - high.astype(F32)).astype(BF16)
    return high, low


def apply(w, u):
    high, low = split(u)
    return jnp.dot(w, jnp.concatenate([high, low, high, low], axis=0), preferred_element_type=F32)


def pack(doubled):
    high, low = split(doubled)
    return jnp.concatenate([high, low], axis=1)


def double(a):
    return jnp.concatenate([a, a], axis=1)


def dot(a, b):
    return jnp.dot(a, b, precision=PRECISE, preferred_element_type=F32)


def growth(x):
    series = 1.0 + x * (1 / 2 + x * (1 / 6 + x * (1 / 24 + x * (1 / 120 + x * (
        1 / 720 + x * (1 / 5040 + x * (1 / 40320)))))))
    small = jnp.abs(x) < 0.5
    safe = jnp.where(small, 1.0, x)
    return jnp.where(small, series, (jnp.exp(x) - 1.0) / safe)


def iota(shape, axis):
    return lax.broadcasted_iota(jnp.int32, shape, axis)


def column(row):
    n = row.shape[1]
    eye = iota((n, n), 0) == iota((n, n), 1)
    return jnp.sum(jnp.where(eye, row, jnp.zeros_like(row)), axis=1, keepdims=True)


def biggest(u):
    used = iota((S, T), 0) < CODONS
    return jnp.max(jnp.where(used, u, 0.0), axis=0, keepdims=True)


def inverse(row):
    return pltpu.reciprocal(row, approx=True)


def held_integrals(basis2, lam2, lam_col, t):
    spread = (lam_col - lam2) * t
    return pack(basis2 * (t * jnp.exp(lam2 * t) * growth(spread)))


def local_children(parents, node):
    late, early = jnp.int32(0), jnp.int32(0)
    for c in range(LOC):
        hit = parents[c] == node
        early = jnp.where(hit, late, early)
        late = jnp.where(hit, c, late)
    return late, early


def slot_of(x, z, c):
    return c * (NX * NZ) + z * NX + x


def prepare(parents_h, lengths_h, top_lengths_h, top_parents_h, tips_h, vectors_h, inverse_h, lam_h, rates_h, freq_h,
            msg, w_top, w_loc, m_loc, y_loc, links, eig_w, inv_w, basis_out, lam_out, freq_out,
            parents, lengths, top_lengths, top_parents, tips, vectors, inverse_vectors, lam, rates, freq, x_int,
            in_sem, send_sem, recv_sem):
    me = lax.axis_index("leaf")
    site = lax.axis_index("site")
    core = lax.rem(me, 2)
    z = lax.rem(me // 2, NZ)
    x = me // (2 * NZ)

    loads = [pltpu.make_async_copy(src, dst, in_sem.at[i]) for i, (src, dst) in enumerate((
        (vectors_h, vectors), (inverse_h, inverse_vectors), (lam_h, lam), (lengths_h, lengths),
        (top_lengths_h, top_lengths), (tips_h, tips), (parents_h, parents), (rates_h, rates),
        (top_parents_h, top_parents), (freq_h, freq)))]
    for load in loads:
        load.start()

    def device(dx, dz, dc):
        nx, nz = lax.rem(x + dx + NX, NX), lax.rem(z + dz + NZ, NZ)
        nc = 1 - core if dc else core
        return ((nx * NZ + nz) * 2 + nc, site)

    x_peers = [(dx, 0, 0) for dx in (1, 2, 3)]
    partners = x_peers + [(0, dz, 0) for dz in range(1, NZ)] + [(0, 0, 1)]
    barrier = pltpu.get_barrier_semaphore()
    for partner in partners:
        pl.semaphore_signal(barrier, inc=1, device_id=device(*partner), device_id_type=MESH)

    for load in loads[:7]:
        load.wait()
    lam_row = lam[...]
    lam_col = column(lam_row)
    lam2 = double(lam_row)
    used = iota((S, S), 0) < CODONS
    right = jnp.where(used, vectors[...], 0.0)
    left = inverse_vectors[...]
    right2 = double(right)
    left_high, left_low = split(double(left))
    left_stack = jnp.concatenate([left_high, left_low, left_high, left_low], axis=0)
    r2, c2 = iota((S, T), 0), iota((S, T), 1)
    eye2 = jnp.where((r2 < CODONS) & ((r2 == c2) | (r2 + S == c2)), 1.0, 0.0)

    def branches(ts):
        scaled = []
        for t in ts:
            arg = lam2 * t
            scaled.append(pack(right2 * (arg * growth(arg))))
        result = jnp.dot(jnp.concatenate(scaled, axis=0), left_stack, preferred_element_type=F32)
        return [pack(eye2 + result[S * i:S * (i + 1)]) for i in range(len(ts))]

    for c, w in enumerate(branches([lengths[c] for c in range(LEAVES)])):
        w_loc[c] = w
        m_loc[c] = apply(w, tips[c])
    inner = branches([lengths[c] for c in range(LEAVES, LOC)] + [top_lengths[me]])
    for c, w in enumerate(inner):
        w_loc[LEAVES + c] = w
    factors = []
    for n in range(LEAVES, LOC + 1):
        a, b = local_children(parents, n)
        u = m_loc[a] * m_loc[b]
        r = inverse(biggest(u))
        factors.append(r)
        x_int[n - LEAVES] = u * r
        y = apply(w_loc[n], u) * r
        if n < LOC:
            m_loc[n] = y
        else:
            logs = -jnp.sum(jnp.log(jnp.concatenate(factors, axis=0)), axis=0, keepdims=True)
            msg[slot_of(x, z, core)] = jnp.where(iota((S, T), 0) == S - 1, logs, y)
    pl.semaphore_wait(barrier, len(partners))

    counter = [0]

    main, rest = pl.ds(0, S - ACROSS), pl.ds(S - ACROSS, ACROSS)

    def block(bx, bz, bc, rows):
        return msg.at[slot_of(bx, bz, bc), rows]

    def group(bz, bc, rows):
        return msg.at[pl.ds(slot_of(0, bz, bc), NX), rows]

    started = []

    def send(piece, where, arriving):
        k = counter[0]
        counter[0] += 1
        copy = pltpu.make_async_remote_copy(src_ref=piece, dst_ref=piece, send_sem=send_sem.at[k],
                                            recv_sem=recv_sem.at[k], device_id=device(*where), device_id_type=MESH)
        copy.start()
        started.append(copy)
        incoming = pltpu.make_async_remote_copy(src_ref=arriving, dst_ref=arriving, send_sem=send_sem.at[k],
                                                recv_sem=recv_sem.at[k], device_id=device(*where), device_id_type=MESH)
        return incoming

    def at_z(dz):
        return lax.rem(z + dz + NZ, NZ)

    def at_x(dx):
        return lax.rem(x + dx + NX, NX)

    def along_z(dz):
        return send(block(x, z, core, main), (0, dz, 0), block(x, at_z(-dz), core, main))

    def along_x(dz, rows):
        return [send(block(x, at_z(-dz), core, rows), (dx, 0, 0), block(at_x(-dx), at_z(-dz), core, rows))
                for dx in (1, 3, 2)]

    def group_z(dz):
        return send(group(z, core, rest), (0, dz, 0), group(at_z(-dz), core, rest))

    def across(dz, rows):
        return send(group(at_z(-dz), core, rows), (0, 0, 1), group(at_z(-dz), 1 - core, rows))

    def shared():
        loads[7].wait()
        loads[8].wait()
        loads[9].wait()
        parent_col = column(top_parents[...])
        child = iota((TOP, T), 0)
        hit = parent_col == iota((TOP, T), 1)
        late = jnp.max(jnp.where(hit, child, 0), axis=0, keepdims=True)
        early = jnp.min(jnp.where(hit, child, TOP), axis=0, keepdims=True)
        pair = jnp.concatenate([late, early, jnp.zeros((6, T), jnp.int32)], axis=0)
        slots = (pair & 1) * (NX * NZ) + ((pair >> 1) & (NZ - 1)) * NX + (pair >> 4)
        pair = jnp.where(pair < GROUPS, slots, pair)
        lane = iota((8, T), 1)
        links[...] = jnp.where((lane >= GROUPS) & (lane <= ROOT), pair, 0)
        freq_out[...] = jnp.broadcast_to(column(freq[...]), (S, T))
        lam_out[...] = jnp.broadcast_to(lam2, (8, T))
        basis_out[...] = double(dot(dot(left, rates[...]), right))
        eig_w[...] = pack(right2)
        inv_w[...] = pack(double(left))

    def products(lo, hi):
        for c in range(lo, hi):
            t = lengths[c] if c < LOC else top_lengths[me]
            v = apply(inv_w[...], tips[c] if c < LEAVES else x_int[c - LEAVES])
            y_loc[c] = apply(eig_w[...], apply(held_integrals(basis_out[...], lam2, lam_col, t), v))

    def matrices(lo, hi):
        def some(i, _):
            ts = [top_lengths[jnp.minimum(GROUPS + i * 8 + j, TOP - 1)] for j in range(8)]
            for j, w in enumerate(branches(ts)):
                w_top[i * 8 + j] = w
            return 0

        lax.fori_loop(lo, hi, some, 0)

    order = (1, -1, 2, -2, 3, -3, 4)
    turns = (0,) + order
    first = along_x(0, rest)
    from_z = {dz: along_z(dz) for dz in order[:2]}
    from_x = {0: along_x(0, main)}
    from_z.update({dz: along_z(dz) for dz in order[2:]})
    crossed = []
    closed = [0]

    def close():
        dz = turns[closed[0]]
        closed[0] += 1
        for one in from_x[dz]:
            one.wait_recv()
        crossed.append(across(dz, main))

    shared()
    for i, dz in enumerate(order):
        from_z[dz].wait_recv()
        from_x[dz] = along_x(dz, main)
        if i == 0:
            for one in first:
                one.wait_recv()
            groups = {d: group_z(d) for d in order}
            crossed.append(across(0, rest))
        if i >= 5:
            close()
        if i in (1, 3, 5):
            matrices(i - 1, i + 1)
    products(0, 5)
    for i, dz in enumerate(order):
        groups[dz].wait_recv()
        crossed.append(across(dz, rest))
        if closed[0] < len(turns):
            close()
        if i == 1:
            products(5, 10)
        if i == 3:
            products(10, 15)
        if i == 5:
            matrices(6, 8)
    while closed[0] < len(turns):
        close()
    for one in crossed:
        one.wait_recv()
    for one in started:
        one.wait_send()


COPIES = 3 * (NZ + 1) + 2 * (NZ - 1) + 2 * NZ


def joining(top_parents_h, top_lengths_h, links, msg_in, w_top, handed, info, factor, msg,
            top_parents, top_lengths, path, arrs, sem):
    del msg_in
    loads = [pltpu.make_async_copy(src, dst, sem.at[i]) for i, (src, dst) in enumerate((
        (top_parents_h, top_parents), (top_lengths_h, top_lengths)))]
    for load in loads:
        load.start()
    me = lax.axis_index("leaf")
    slot = slot_of(me // (2 * NZ), lax.rem(me // 2, NZ), lax.rem(me, 2))
    factor[...] = jnp.ones((72, T), F32)
    def late(n):
        return links[0, n]

    def early(n):
        return links[1, n]

    def climb(n):
        done = []
        fits = True
        steps = jnp.int32(1)
        for j in range(WIN):
            k = jnp.minimum(n + j, T - 1) if j > 1 else n + j
            a, b = late(k), early(k)
            if j:
                fits = fits & (a < n)
                steps = steps + fits.astype(jnp.int32)
            u = msg[a] * msg[b]
            y = apply(w_top[jnp.minimum(k, ROOT) - GROUPS], u)
            r = inverse(biggest(u))
            done.append((y * r, r))
        for j, (y, r) in enumerate(done):
            msg[n + j] = y
            factor[pl.ds(n + j - GROUPS, 1)] = r
        return n + steps

    lax.while_loop(lambda n: n < ROOT, climb, jnp.int32(GROUPS))

    for load in loads:
        load.wait()

    def walk(state):
        c, depth, mine, at = state
        path[depth] = c
        p = top_parents[jnp.where(depth == 0, me, c)]
        found = (mine < 0) & (late(p) == c)
        return (p, depth + 1, jnp.where(found, p, mine), jnp.where(found, depth + 1, at))

    _, depth, mine, at = lax.while_loop(
        lambda state: state[0] != ROOT, walk, (slot, jnp.int32(0), jnp.int32(-1), jnp.int32(0)))
    counted = (mine >= 0) & (mine < ROOT)
    node = jnp.where(counted, mine, GROUPS)
    at = jnp.where(counted, at, 0)

    def step_down(i, o):
        k = depth - 1 - i
        c = path[k]
        p = top_parents[c]
        arriving = o * msg[late(p) + early(p) - c]
        arrs[k] = arriving
        return apply(w_top[c - GROUPS], arriving) * inverse(biggest(arriving))

    o = lax.fori_loop(0, depth - 1, step_down, jnp.ones((S, T), F32))
    p = top_parents[me]
    leaf_arriving = o * msg[late(p) + early(p) - slot]
    arrs[0] = leaf_arriving
    handed[0] = leaf_arriving
    handed[1] = msg[slot]
    handed[2] = arrs[at]
    handed[3] = msg[node]
    handed[4] = msg[late(node)] * msg[early(node)] * factor[pl.ds(node - GROUPS, 1)]
    handed[5] = msg[late(ROOT)] * msg[early(ROOT)]
    row = iota((8, T), 0)
    info[...] = jnp.where(row == 0, top_lengths[node], jnp.where(counted, node, -1).astype(F32))


PHASES = ("yc", "x", "z")


def tail(parents_h, weights_h, handed, info, factor, msg, w_loc, m_loc, y_loc, eig_w, inv_w, basis, lam, freq, out,
         parents, weights, o_loc, rows, *rest):
    bufs, parts = rest[:len(PHASES)], rest[len(PHASES):2 * len(PHASES)]
    in_sem, send_sem, recv_sem = rest[2 * len(PHASES):]
    loads = [pltpu.make_async_copy(parents_h, parents, in_sem.at[0]), pltpu.make_async_copy(weights_h, weights, in_sem.at[1])]
    for load in loads:
        load.start()
    me = lax.axis_index("leaf")
    sizes = {"x": NX, "z": NZ, "c": 2, "y": lax.axis_size("site")}
    here = {"x": me // (2 * NZ), "z": lax.rem(me // 2, NZ), "c": lax.rem(me, 2), "y": lax.axis_index("site")}

    def shifted(offset):
        return {a: (lax.rem(here[a] + offset.get(a, 0) + sizes[a], sizes[a])) for a in here}

    def device(offset):
        at = shifted(offset)
        return ((at["x"] * NZ + at["z"]) * 2 + at["c"], at["y"])

    def place(axes, at):
        index = 0
        for a in axes:
            index = index * sizes[a] + at[a]
        return index

    offsets = [phase_offsets(axes, sizes) for axes in PHASES]
    barrier = pltpu.get_barrier_semaphore()
    for some in offsets:
        for offset in some:
            pl.semaphore_signal(barrier, inc=1, device_id=device(offset), device_id_type=MESH)

    freq_col = freq[...]

    def ratio(row, arriving, message, y):
        weighted = freq_col * arriving
        rows[0, pl.ds(row, 1)] = jnp.sum(weighted * y, axis=0, keepdims=True)
        rows[1, pl.ds(row, 1)] = jnp.sum(weighted * message, axis=0, keepdims=True)

    rows[...] = jnp.ones((2, 24, T), F32)
    lam2 = lam[0:1]
    o_loc[LOC - LEAVES] = apply(w_loc[LOC], handed[0]) * inverse(biggest(handed[0]))
    ratio(16, handed[0], handed[1], y_loc[LOC])
    held = held_integrals(basis[...], lam2, column(lam2[:, :S]), info[0:1, 0:1])
    ratio(17, handed[2], handed[3], apply(eig_w[...], apply(held, apply(inv_w[...], handed[4]))))
    for load in loads:
        load.wait()
    for c in range(LOC - 1, -1, -1):
        p = jnp.clip(parents[c], LEAVES, LOC)
        sibling = jnp.int32(0)
        for other in range(LOC):
            if other != c:
                sibling = jnp.where(parents[other] == p, other, sibling)
        arriving = o_loc[p - LEAVES] * m_loc[sibling]
        if c >= LEAVES:
            o_loc[c - LEAVES] = apply(w_loc[c], arriving) * inverse(biggest(arriving))
        ratio(c, arriving, m_loc[c], y_loc[c])
    weight = weights[...].astype(F32)
    expected = jnp.where(iota((24, T), 0) == LOC, weight, weight * rows[0] / rows[1])
    expected = jnp.concatenate([expected, jnp.zeros((T - 24, T), F32)], axis=0)
    sums = lax.dot_general(jnp.ones((8, T), F32), expected, (((1,), (1,)), ((), ())),
                           precision=PRECISE, preferred_element_type=F32)
    lane = iota((1, T), 1)
    node = info[1:2]
    top_row = jnp.where(lane == me, sums[0:1, 16:17], 0.0) + jnp.where(lane.astype(F32) == node, sums[0:1, 17:18], 0.0)
    parts[0][...] = jnp.concatenate([sums[0:1], top_row], axis=0)

    logs = [msg[g, pl.ds(S - 1, 1)] for g in range(GROUPS)]
    while len(logs) > 1:
        logs = [a + b for a, b in zip(logs[::2], logs[1::2])]
    inner = -jnp.sum(jnp.log(jnp.where(iota((72, T), 0) < TOP - GROUPS, factor[...], 1.0)), axis=0, keepdims=True)
    likelihood = jnp.sum(freq_col * handed[5], axis=0, keepdims=True)
    loglik = (jnp.log(likelihood) + inner + logs[0]) * (1.0 / (GROUPS * LEAVES))
    pl.semaphore_wait(barrier, sum(map(len, offsets)))

    k = 0
    copies = []
    for i, (axes, some) in enumerate(zip(PHASES, offsets)):
        buf, part = bufs[i], parts[i]
        mine = place(axes, here)
        buf[mine] = part[...]
        arrivals = []
        for offset in some:
            copy = pltpu.make_async_remote_copy(src_ref=part, dst_ref=buf.at[mine], send_sem=send_sem.at[k],
                                                recv_sem=recv_sem.at[k], device_id=device(offset), device_id_type=MESH)
            copy.start()
            copies.append(copy)
            there = buf.at[place(axes, shifted({a: -n for a, n in offset.items()}))]
            arrivals.append(pltpu.make_async_remote_copy(
                src_ref=there, dst_ref=there, send_sem=send_sem.at[k], recv_sem=recv_sem.at[k],
                device_id=device(offset), device_id_type=MESH))
            k += 1
        for arrival in arrivals:
            arrival.wait_recv()
        if i == 0:
            local = buf[here["c"], 0:1]
            total = buf[0, 1:2] + buf[1, 1:2]
            for n in range(1, sizes["y"]):
                local = local + buf[2 * n + here["c"], 0:1]
                total = total + (buf[2 * n, 1:2] + buf[2 * n + 1, 1:2])
            weight_total = local[:, LOC:LOC + 1]
        else:
            total = buf[0]
            for n in range(1, len(some) + 1):
                total = total + buf[n]
        if i + 1 < len(PHASES):
            parts[i + 1][...] = total
    out[...] = jnp.concatenate([local / weight_total, total / weight_total, loglik], axis=0)
    for copy in copies:
        copy.wait_send()


def finish(rows, local, top, loglik):
    local[...] = rows[0:1, :LOC]
    top[...] = rows[1:2, :TOP]
    loglik[...] = rows[2:3]


def phase_offsets(axes, sizes):
    found = [{}]
    for a in axes:
        found = [{**one, a: n} for one in found for n in range(sizes[a])]
    return [one for one in found if any(one.values())]


def on_device(tips, parents, branch_lengths, top_parents, top_lengths, weights, eig_vectors,
              eig_inverse, eig_values, labeled_rates, root_freq):
    hbm = pl.BlockSpec(memory_space=pltpu.HBM)
    stay = functools.partial(pltpu.with_memory_space_constraint, memory_space=pltpu.HBM)
    smem = pl.BlockSpec(memory_space=pltpu.SMEM)
    vmem = pl.BlockSpec(memory_space=pltpu.VMEM)
    shape = jax.ShapeDtypeStruct
    msg, *made = pl.pallas_call(
        prepare,
        out_shape=(
            shape((ROOT + 1 + WIN, S, T), F32),
            shape((GROUPS, S, 256), BF16),
            shape((LOC + 1, S, 256), BF16),
            shape((LOC, S, T), F32),
            shape((LOC + 1, S, T), F32),
            shape((8, T), jnp.int32),
            shape((S, 256), BF16),
            shape((S, 256), BF16),
            shape((S, T), F32),
            shape((8, T), F32),
            shape((S, T), F32),
        ),
        in_specs=[hbm] * 10,
        out_specs=(vmem,) * 11,
        scratch_shapes=[
            pltpu.SMEM((LOC,), jnp.int32),
            pltpu.SMEM((LOC,), F32),
            pltpu.SMEM((TOP,), F32),
            pltpu.VMEM((1, TOP), jnp.int32),
            pltpu.VMEM((LEAVES, S, T), F32),
            pltpu.VMEM((S, S), F32),
            pltpu.VMEM((S, S), F32),
            pltpu.VMEM((1, S), F32),
            pltpu.VMEM((S, S), F32),
            pltpu.VMEM((1, S), F32),
            pltpu.VMEM((8, S, T), F32),
            pltpu.SemaphoreType.DMA((10,)),
            pltpu.SemaphoreType.DMA((COPIES,)),
            pltpu.SemaphoreType.DMA((COPIES,)),
        ],
        compiler_params=pltpu.CompilerParams(vmem_limit_bytes=40 << 20, collective_id=0, has_side_effects=True),
        name="prepare",
    )(*map(stay, (parents, branch_lengths, top_lengths, top_parents.reshape(1, TOP), tips, eig_vectors, eig_inverse,
                   eig_values.reshape(1, S), labeled_rates, root_freq.reshape(1, S))))
    w_top, w_loc, m_loc, y_loc, links, eig_w, inv_w, basis, lam, freq = made
    handed, info, factor, msg = pl.pallas_call(
        joining,
        out_shape=(shape((6, S, T), F32), shape((8, T), F32), shape((72, T), F32), shape(msg.shape, F32)),
        in_specs=[hbm] * 2 + [smem] + [vmem] * 2,
        out_specs=(vmem,) * 4,
        input_output_aliases={3: 3},
        scratch_shapes=[
            pltpu.SMEM((TOP,), jnp.int32),
            pltpu.SMEM((TOP,), F32),
            pltpu.SMEM((64,), jnp.int32),
            pltpu.VMEM((GROUPS, S, T), F32),
            pltpu.SemaphoreType.DMA((2,)),
        ],
        compiler_params=pltpu.CompilerParams(vmem_limit_bytes=24 << 20),
        name="joining",
    )(*map(stay, (top_parents, top_lengths)), links, msg, w_top)
    sizes = {"x": NX, "z": NZ, "c": 2, "y": lax.axis_size("site")}
    offsets = [phase_offsets(axes, sizes) for axes in PHASES]
    count = sum(map(len, offsets))
    rows = pl.pallas_call(
        tail,
        out_shape=shape((3, T), F32),
        in_specs=[hbm] * 2 + [vmem] * 12,
        out_specs=vmem,
        scratch_shapes=[
            pltpu.SMEM((LOC,), jnp.int32),
            pltpu.VMEM((1, T), jnp.int32),
            pltpu.VMEM((8, S, T), F32),
            pltpu.VMEM((2, 24, T), F32),
        ] + [pltpu.VMEM((len(some) + 1, 1 if i else 2, T), F32) for i, some in enumerate(offsets)] + [
            pltpu.VMEM((1 if i else 2, T), F32) for i in range(len(offsets))] + [
            pltpu.SemaphoreType.DMA((2,)),
            pltpu.SemaphoreType.DMA((count,)),
            pltpu.SemaphoreType.DMA((count,)),
        ],
        compiler_params=pltpu.CompilerParams(vmem_limit_bytes=24 << 20, collective_id=1, has_side_effects=True),
        name="tail",
    )(*map(stay, (parents, weights.reshape(1, T))), handed, info, factor, msg, w_loc, m_loc, y_loc, eig_w, inv_w, basis, lam, freq)
    local, top, loglik = pl.pallas_call(
        finish,
        out_shape=(shape((1, LOC), F32), shape((1, TOP), F32), shape((1, T), F32)),
        in_specs=[vmem],
        out_specs=(vmem,) * 3,
        compiler_params=pltpu.CompilerParams(vmem_limit_bytes=4 << 20),
        name="finish",
    )(rows)
    return local.reshape(LOC), top.reshape(TOP), loglik.reshape(T)


def solution(mesh):
    placed = (P("leaf", None, "site"), P("leaf"), P("leaf"), P(), P(), P("site"), P(), P(), P(), P(), P())
    return jax.shard_map(
        on_device,
        mesh=mesh,
        in_specs=placed,
        out_specs=(P("leaf"), P(), P("site")),
        check_vma=False,
    )
```

```python
import functools

import jax
import jax.numpy as jnp
from jax import lax
from jax.experimental import pallas as pl
from jax.experimental.pallas import tpu as pltpu
from jax.sharding import PartitionSpec as P

CODONS = 61
S = 64
T = 128
LEAVES = 8
LOC = 14
GROUPS = 64
TOP = 126
ROOT = 126
WIN = 6
ACROSS = 16
F32 = jnp.float32
BF16 = jnp.bfloat16
PRECISE = lax.Precision.HIGHEST
NX, NZ = 4, 8
MESH = pl.DeviceIdType.MESH


def split(u):
    high = u.astype(BF16)
    low = (u - high.astype(F32)).astype(BF16)
    return high, low


def apply(w, u):
    high, low = split(u)
    return jnp.dot(w, jnp.concatenate([high, low, high, low], axis=0), preferred_element_type=F32)


def pack(doubled):
    high, low = split(doubled)
    return jnp.concatenate([high, low], axis=1)


def double(a):
    return jnp.concatenate([a, a], axis=1)


def dot(a, b):
    return jnp.dot(a, b, precision=PRECISE, preferred_element_type=F32)


def growth(x):
    series = 1.0 + x * (1 / 2 + x * (1 / 6 + x * (1 / 24 + x * (1 / 120 + x * (
        1 / 720 + x * (1 / 5040 + x * (1 / 40320)))))))
    small = jnp.abs(x) < 0.5
    safe = jnp.where(small, 1.0, x)
    return jnp.where(small, series, (jnp.exp(x) - 1.0) / safe)


def iota(shape, axis):
    return lax.broadcasted_iota(jnp.int32, shape, axis)


def column(row):
    n = row.shape[1]
    eye = iota((n, n), 0) == iota((n, n), 1)
    return jnp.sum(jnp.where(eye, row, jnp.zeros_like(row)), axis=1, keepdims=True)


def biggest(u):
    used = iota((S, T), 0) < CODONS
    return jnp.max(jnp.where(used, u, 0.0), axis=0, keepdims=True)


def inverse(row):
    return pltpu.reciprocal(row, approx=True)


def held_integrals(basis2, lam2, lam_col, t):
    spread = (lam_col - lam2) * t
    return pack(basis2 * (t * jnp.exp(lam2 * t) * growth(spread)))


def local_children(parents, node):
    late, early = jnp.int32(0), jnp.int32(0)
    for c in range(LOC):
        hit = parents[c] == node
        early = jnp.where(hit, late, early)
        late = jnp.where(hit, c, late)
    return late, early


def slot_of(x, z, c):
    return c * (NX * NZ) + z * NX + x


def prepare(parents_h, lengths_h, top_lengths_h, top_parents_h, tips_h, vectors_h, inverse_h, lam_h, rates_h, freq_h,
            msg, w_top, w_loc, m_loc, y_loc, links, eig_w, inv_w, basis_out, lam_out, freq_out,
            parents, lengths, top_lengths, top_parents, tips, vectors, inverse_vectors, lam, rates, freq, x_int,
            in_sem, send_sem, recv_sem):
    me = lax.axis_index("leaf")
    site = lax.axis_index("site")
    core = lax.rem(me, 2)
    z = lax.rem(me // 2, NZ)
    x = me // (2 * NZ)

    loads = [pltpu.make_async_copy(src, dst, in_sem.at[i]) for i, (src, dst) in enumerate((
        (vectors_h, vectors), (inverse_h, inverse_vectors), (lam_h, lam), (lengths_h, lengths),
        (top_lengths_h, top_lengths), (tips_h, tips), (parents_h, parents), (rates_h, rates),
        (top_parents_h, top_parents), (freq_h, freq)))]
    for load in loads:
        load.start()

    def device(dx, dz, dc):
        nx, nz = lax.rem(x + dx + NX, NX), lax.rem(z + dz + NZ, NZ)
        nc = 1 - core if dc else core
        return ((nx * NZ + nz) * 2 + nc, site)

    x_peers = [(dx, 0, 0) for dx in (1, 2, 3)]
    partners = x_peers + [(0, dz, 0) for dz in range(1, NZ)] + [(0, 0, 1)]
    barrier = pltpu.get_barrier_semaphore()
    for partner in partners:
        pl.semaphore_signal(barrier, inc=1, device_id=device(*partner), device_id_type=MESH)

    for load in loads[:7]:
        load.wait()
    lam_row = lam[...]
    lam_col = column(lam_row)
    lam2 = double(lam_row)
    used = iota((S, S), 0) < CODONS
    right = jnp.where(used, vectors[...], 0.0)
    left = inverse_vectors[...]
    right2 = double(right)
    left_high, left_low = split(double(left))
    left_stack = jnp.concatenate([left_high, left_low, left_high, left_low], axis=0)
    r2, c2 = iota((S, T), 0), iota((S, T), 1)
    eye2 = jnp.where((r2 < CODONS) & ((r2 == c2) | (r2 + S == c2)), 1.0, 0.0)

    def branches(ts):
        scaled = []
        for t in ts:
            arg = lam2 * t
            scaled.append(pack(right2 * (arg * growth(arg))))
        result = jnp.dot(jnp.concatenate(scaled, axis=0), left_stack, preferred_element_type=F32)
        return [pack(eye2 + result[S * i:S * (i + 1)]) for i in range(len(ts))]

    for c, w in enumerate(branches([lengths[c] for c in range(LEAVES)])):
        w_loc[c] = w
        m_loc[c] = apply(w, tips[c])
    inner = branches([lengths[c] for c in range(LEAVES, LOC)] + [top_lengths[me]])
    for c, w in enumerate(inner):
        w_loc[LEAVES + c] = w
    factors = []
    for n in range(LEAVES, LOC + 1):
        a, b = local_children(parents, n)
        u = m_loc[a] * m_loc[b]
        r = inverse(biggest(u))
        factors.append(r)
        x_int[n - LEAVES] = u * r
        y = apply(w_loc[n], u) * r
        if n < LOC:
            m_loc[n] = y
        else:
            logs = -jnp.sum(jnp.log(jnp.concatenate(factors, axis=0)), axis=0, keepdims=True)
            msg[slot_of(x, z, core)] = jnp.where(iota((S, T), 0) == S - 1, logs, y)
    pl.semaphore_wait(barrier, len(partners))

    counter = [0]

    main, rest = pl.ds(0, S - ACROSS), pl.ds(S - ACROSS, ACROSS)

    def block(bx, bz, bc, rows):
        return msg.at[slot_of(bx, bz, bc), rows]

    def group(bz, bc, rows):
        return msg.at[pl.ds(slot_of(0, bz, bc), NX), rows]

    started = []

    def send(piece, where, arriving):
        k = counter[0]
        counter[0] += 1
        copy = pltpu.make_async_remote_copy(src_ref=piece, dst_ref=piece, send_sem=send_sem.at[k],
                                            recv_sem=recv_sem.at[k], device_id=device(*where), device_id_type=MESH)
        copy.start()
        started.append(copy)
        incoming = pltpu.make_async_remote_copy(src_ref=arriving, dst_ref=arriving, send_sem=send_sem.at[k],
                                                recv_sem=recv_sem.at[k], device_id=device(*where), device_id_type=MESH)
        return incoming

    def at_z(dz):
        return lax.rem(z + dz + NZ, NZ)

    def at_x(dx):
        return lax.rem(x + dx + NX, NX)

    def along_z(dz):
        return send(block(x, z, core, main), (0, dz, 0), block(x, at_z(-dz), core, main))

    def along_x(dz, rows):
        return [send(block(x, at_z(-dz), core, rows), (dx, 0, 0), block(at_x(-dx), at_z(-dz), core, rows))
                for dx in (1, 3, 2)]

    def group_z(dz):
        return send(group(z, core, rest), (0, dz, 0), group(at_z(-dz), core, rest))

    def across(dz, rows):
        return send(group(at_z(-dz), core, rows), (0, 0, 1), group(at_z(-dz), 1 - core, rows))

    def shared():
        loads[7].wait()
        loads[8].wait()
        loads[9].wait()
        parent_col = column(top_parents[...])
        child = iota((TOP, T), 0)
        hit = parent_col == iota((TOP, T), 1)
        late = jnp.max(jnp.where(hit, child, 0), axis=0, keepdims=True)
        early = jnp.min(jnp.where(hit, child, TOP), axis=0, keepdims=True)
        pair = jnp.concatenate([late, early, jnp.zeros((6, T), jnp.int32)], axis=0)
        slots = (pair & 1) * (NX * NZ) + ((pair >> 1) & (NZ - 1)) * NX + (pair >> 4)
        pair = jnp.where(pair < GROUPS, slots, pair)
        lane = iota((8, T), 1)
        links[...] = jnp.where((lane >= GROUPS) & (lane <= ROOT), pair, 0)
        freq_out[...] = jnp.broadcast_to(column(freq[...]), (S, T))
        lam_out[...] = jnp.broadcast_to(lam2, (8, T))
        basis_out[...] = double(dot(dot(left, rates[...]), right))
        eig_w[...] = pack(right2)
        inv_w[...] = pack(double(left))

    def products(lo, hi):
        for c in range(lo, hi):
            t = lengths[c] if c < LOC else top_lengths[me]
            v = apply(inv_w[...], tips[c] if c < LEAVES else x_int[c - LEAVES])
            y_loc[c] = apply(eig_w[...], apply(held_integrals(basis_out[...], lam2, lam_col, t), v))

    def matrices(lo, hi):
        def some(i, _):
            ts = [top_lengths[jnp.minimum(GROUPS + i * 8 + j, TOP - 1)] for j in range(8)]
            for j, w in enumerate(branches(ts)):
                w_top[i * 8 + j] = w
            return 0

        lax.fori_loop(lo, hi, some, 0)

    order = (1, -1, 2, -2, 3, -3, 4)
    turns = (0,) + order
    first = along_x(0, rest)
    from_z = {dz: along_z(dz) for dz in order[:2]}
    from_x = {0: along_x(0, main)}
    from_z.update({dz: along_z(dz) for dz in order[2:]})
    crossed = []
    closed = [0]

    def close():
        dz = turns[closed[0]]
        closed[0] += 1
        for one in from_x[dz]:
            one.wait_recv()
        crossed.append(across(dz, main))

    shared()
    products(0, 5)
    for i, dz in enumerate(order):
        from_z[dz].wait_recv()
        from_x[dz] = along_x(dz, main)
        if i == 0:
            for one in first:
                one.wait_recv()
            groups = {d: group_z(d) for d in order}
            crossed.append(across(0, rest))
        if i >= 5:
            close()
        if i in (1, 3, 5):
            matrices(i - 1, i + 1)
    for i, dz in enumerate(order):
        groups[dz].wait_recv()
        crossed.append(across(dz, rest))
        if closed[0] < len(turns):
            close()
        if i == 1:
            products(5, 10)
        if i == 3:
            products(10, 15)
        if i == 5:
            matrices(6, 8)
    while closed[0] < len(turns):
        close()
    for one in crossed:
        one.wait_recv()
    for one in started:
        one.wait_send()


COPIES = 3 * (NZ + 1) + 2 * (NZ - 1) + 2 * NZ


def joining(top_parents_h, top_lengths_h, links, msg_in, w_top, handed, info, factor, msg,
            top_parents, top_lengths, path, arrs, sem):
    del msg_in
    loads = [pltpu.make_async_copy(src, dst, sem.at[i]) for i, (src, dst) in enumerate((
        (top_parents_h, top_parents), (top_lengths_h, top_lengths)))]
    for load in loads:
        load.start()
    me = lax.axis_index("leaf")
    slot = slot_of(me // (2 * NZ), lax.rem(me // 2, NZ), lax.rem(me, 2))
    factor[...] = jnp.ones((72, T), F32)
    def late(n):
        return links[0, n]

    def early(n):
        return links[1, n]

    def climb(n):
        done = []
        fits = True
        steps = jnp.int32(1)
        for j in range(WIN):
            k = jnp.minimum(n + j, T - 1) if j > 1 else n + j
            a, b = late(k), early(k)
            if j:
                fits = fits & (a < n)
                steps = steps + fits.astype(jnp.int32)
            u = msg[a] * msg[b]
            y = apply(w_top[jnp.minimum(k, ROOT) - GROUPS], u)
            r = inverse(biggest(u))
            done.append((y * r, r))
        for j, (y, r) in enumerate(done):
            msg[n + j] = y
            factor[pl.ds(n + j - GROUPS, 1)] = r
        return n + steps

    lax.while_loop(lambda n: n < ROOT, climb, jnp.int32(GROUPS))

    for load in loads:
        load.wait()

    def walk(state):
        c, depth, mine, at = state
        path[depth] = c
        p = top_parents[jnp.where(depth == 0, me, c)]
        found = (mine < 0) & (late(p) == c)
        return (p, depth + 1, jnp.where(found, p, mine), jnp.where(found, depth + 1, at))

    _, depth, mine, at = lax.while_loop(
        lambda state: state[0] != ROOT, walk, (slot, jnp.int32(0), jnp.int32(-1), jnp.int32(0)))
    counted = (mine >= 0) & (mine < ROOT)
    node = jnp.where(counted, mine, GROUPS)
    at = jnp.where(counted, at, 0)

    def step_down(i, o):
        k = depth - 1 - i
        c = path[k]
        p = top_parents[c]
        arriving = o * msg[late(p) + early(p) - c]
        arrs[k] = arriving
        return apply(w_top[c - GROUPS], arriving) * inverse(biggest(arriving))

    o = lax.fori_loop(0, depth - 1, step_down, jnp.ones((S, T), F32))
    p = top_parents[me]
    leaf_arriving = o * msg[late(p) + early(p) - slot]
    arrs[0] = leaf_arriving
    handed[0] = leaf_arriving
    handed[1] = msg[slot]
    handed[2] = arrs[at]
    handed[3] = msg[node]
    handed[4] = msg[late(node)] * msg[early(node)] * factor[pl.ds(node - GROUPS, 1)]
    handed[5] = msg[late(ROOT)] * msg[early(ROOT)]
    row = iota((8, T), 0)
    info[...] = jnp.where(row == 0, top_lengths[node], jnp.where(counted, node, -1).astype(F32))


PHASES = ("y", "cx", "z")


def tail(parents_h, weights_h, handed, info, factor, msg, w_loc, m_loc, y_loc, eig_w, inv_w, basis, lam, freq, out,
         parents, weights, o_loc, rows, *rest):
    bufs, parts = rest[:len(PHASES)], rest[len(PHASES):2 * len(PHASES)]
    in_sem, send_sem, recv_sem = rest[2 * len(PHASES):]
    loads = [pltpu.make_async_copy(parents_h, parents, in_sem.at[0]), pltpu.make_async_copy(weights_h, weights, in_sem.at[1])]
    for load in loads:
        load.start()
    me = lax.axis_index("leaf")
    sizes = {"x": NX, "z": NZ, "c": 2, "y": lax.axis_size("site")}
    here = {"x": me // (2 * NZ), "z": lax.rem(me // 2, NZ), "c": lax.rem(me, 2), "y": lax.axis_index("site")}

    def shifted(offset):
        return {a: (lax.rem(here[a] + offset.get(a, 0) + sizes[a], sizes[a])) for a in here}

    def device(offset):
        at = shifted(offset)
        return ((at["x"] * NZ + at["z"]) * 2 + at["c"], at["y"])

    def place(axes, at):
        index = 0
        for a in axes:
            index = index * sizes[a] + at[a]
        return index

    offsets = [phase_offsets(axes, sizes) for axes in PHASES]
    barrier = pltpu.get_barrier_semaphore()
    for some in offsets:
        for offset in some:
            pl.semaphore_signal(barrier, inc=1, device_id=device(offset), device_id_type=MESH)

    freq_col = freq[...]

    def ratio(row, arriving, message, y):
        weighted = freq_col * arriving
        rows[0, pl.ds(row, 1)] = jnp.sum(weighted * y, axis=0, keepdims=True)
        rows[1, pl.ds(row, 1)] = jnp.sum(weighted * message, axis=0, keepdims=True)

    rows[...] = jnp.ones((2, 24, T), F32)
    lam2 = lam[0:1]
    o_loc[LOC - LEAVES] = apply(w_loc[LOC], handed[0]) * inverse(biggest(handed[0]))
    ratio(16, handed[0], handed[1], y_loc[LOC])
    held = held_integrals(basis[...], lam2, column(lam2[:, :S]), info[0:1, 0:1])
    ratio(17, handed[2], handed[3], apply(eig_w[...], apply(held, apply(inv_w[...], handed[4]))))
    for load in loads:
        load.wait()
    for c in range(LOC - 1, -1, -1):
        p = jnp.clip(parents[c], LEAVES, LOC)
        sibling = jnp.int32(0)
        for other in range(LOC):
            if other != c:
                sibling = jnp.where(parents[other] == p, other, sibling)
        arriving = o_loc[p - LEAVES] * m_loc[sibling]
        if c >= LEAVES:
            o_loc[c - LEAVES] = apply(w_loc[c], arriving) * inverse(biggest(arriving))
        ratio(c, arriving, m_loc[c], y_loc[c])
    weight = weights[...].astype(F32)
    expected = jnp.where(iota((24, T), 0) == LOC, weight, weight * rows[0] / rows[1])
    expected = jnp.concatenate([expected, jnp.zeros((T - 24, T), F32)], axis=0)
    sums = lax.dot_general(jnp.ones((8, T), F32), expected, (((1,), (1,)), ((), ())),
                           precision=PRECISE, preferred_element_type=F32)
    lane = iota((1, T), 1)
    node = info[1:2]
    top_row = jnp.where(lane == me, sums[0:1, 16:17], 0.0) + jnp.where(lane.astype(F32) == node, sums[0:1, 17:18], 0.0)
    parts[0][...] = jnp.concatenate([sums[0:1], top_row], axis=0)

    logs = [msg[g, pl.ds(S - 1, 1)] for g in range(GROUPS)]
    while len(logs) > 1:
        logs = [a + b for a, b in zip(logs[::2], logs[1::2])]
    inner = -jnp.sum(jnp.log(jnp.where(iota((72, T), 0) < TOP - GROUPS, factor[...], 1.0)), axis=0, keepdims=True)
    likelihood = jnp.sum(freq_col * handed[5], axis=0, keepdims=True)
    loglik = (jnp.log(likelihood) + inner + logs[0]) * (1.0 / (GROUPS * LEAVES))
    pl.semaphore_wait(barrier, sum(map(len, offsets)))

    k = 0
    copies = []
    for i, (axes, some) in enumerate(zip(PHASES, offsets)):
        buf, part = bufs[i], parts[i]
        mine = place(axes, here)
        buf[mine] = part[...]
        arrivals = []
        for offset in some:
            copy = pltpu.make_async_remote_copy(src_ref=part, dst_ref=buf.at[mine], send_sem=send_sem.at[k],
                                                recv_sem=recv_sem.at[k], device_id=device(offset), device_id_type=MESH)
            copy.start()
            copies.append(copy)
            there = buf.at[place(axes, shifted({a: -n for a, n in offset.items()}))]
            arrivals.append(pltpu.make_async_remote_copy(
                src_ref=there, dst_ref=there, send_sem=send_sem.at[k], recv_sem=recv_sem.at[k],
                device_id=device(offset), device_id_type=MESH))
            k += 1
        for arrival in arrivals:
            arrival.wait_recv()
        if i == 0:
            local, total = buf[0, 0:1], buf[0, 1:2]
            for n in range(1, sizes["y"]):
                local = local + buf[n, 0:1]
                total = total + buf[n, 1:2]
            weight_total = local[:, LOC:LOC + 1]
        else:
            total = buf[0]
            for n in range(1, len(some) + 1):
                total = total + buf[n]
        if i + 1 < len(PHASES):
            parts[i + 1][...] = total
    out[...] = jnp.concatenate([local / weight_total, total / weight_total, loglik], axis=0)
    for copy in copies:
        copy.wait_send()


def finish(rows, local, top, loglik):
    local[...] = rows[0:1, :LOC]
    top[...] = rows[1:2, :TOP]
    loglik[...] = rows[2:3]


def phase_offsets(axes, sizes):
    found = [{}]
    for a in axes:
        found = [{**one, a: n} for one in found for n in range(sizes[a])]
    return [one for one in found if any(one.values())]


def on_device(tips, parents, branch_lengths, top_parents, top_lengths, weights, eig_vectors,
              eig_inverse, eig_values, labeled_rates, root_freq):
    hbm = pl.BlockSpec(memory_space=pltpu.HBM)
    stay = functools.partial(pltpu.with_memory_space_constraint, memory_space=pltpu.HBM)
    smem = pl.BlockSpec(memory_space=pltpu.SMEM)
    vmem = pl.BlockSpec(memory_space=pltpu.VMEM)
    shape = jax.ShapeDtypeStruct
    msg, *made = pl.pallas_call(
        prepare,
        out_shape=(
            shape((ROOT + 1 + WIN, S, T), F32),
            shape((GROUPS, S, 256), BF16),
            shape((LOC + 1, S, 256), BF16),
            shape((LOC, S, T), F32),
            shape((LOC + 1, S, T), F32),
            shape((8, T), jnp.int32),
            shape((S, 256), BF16),
            shape((S, 256), BF16),
            shape((S, T), F32),
            shape((8, T), F32),
            shape((S, T), F32),
        ),
        in_specs=[hbm] * 10,
        out_specs=(vmem,) * 11,
        scratch_shapes=[
            pltpu.SMEM((LOC,), jnp.int32),
            pltpu.SMEM((LOC,), F32),
            pltpu.SMEM((TOP,), F32),
            pltpu.VMEM((1, TOP), jnp.int32),
            pltpu.VMEM((LEAVES, S, T), F32),
            pltpu.VMEM((S, S), F32),
            pltpu.VMEM((S, S), F32),
            pltpu.VMEM((1, S), F32),
            pltpu.VMEM((S, S), F32),
            pltpu.VMEM((1, S), F32),
            pltpu.VMEM((8, S, T), F32),
            pltpu.SemaphoreType.DMA((10,)),
            pltpu.SemaphoreType.DMA((COPIES,)),
            pltpu.SemaphoreType.DMA((COPIES,)),
        ],
        compiler_params=pltpu.CompilerParams(vmem_limit_bytes=40 << 20, collective_id=0, has_side_effects=True),
        name="prepare",
    )(*map(stay, (parents, branch_lengths, top_lengths, top_parents.reshape(1, TOP), tips, eig_vectors, eig_inverse,
                   eig_values.reshape(1, S), labeled_rates, root_freq.reshape(1, S))))
    w_top, w_loc, m_loc, y_loc, links, eig_w, inv_w, basis, lam, freq = made
    handed, info, factor, msg = pl.pallas_call(
        joining,
        out_shape=(shape((6, S, T), F32), shape((8, T), F32), shape((72, T), F32), shape(msg.shape, F32)),
        in_specs=[hbm] * 2 + [smem] + [vmem] * 2,
        out_specs=(vmem,) * 4,
        input_output_aliases={3: 3},
        scratch_shapes=[
            pltpu.SMEM((TOP,), jnp.int32),
            pltpu.SMEM((TOP,), F32),
            pltpu.SMEM((64,), jnp.int32),
            pltpu.VMEM((GROUPS, S, T), F32),
            pltpu.SemaphoreType.DMA((2,)),
        ],
        compiler_params=pltpu.CompilerParams(vmem_limit_bytes=24 << 20),
        name="joining",
    )(*map(stay, (top_parents, top_lengths)), links, msg, w_top)
    sizes = {"x": NX, "z": NZ, "c": 2, "y": lax.axis_size("site")}
    offsets = [phase_offsets(axes, sizes) for axes in PHASES]
    count = sum(map(len, offsets))
    rows = pl.pallas_call(
        tail,
        out_shape=shape((3, T), F32),
        in_specs=[hbm] * 2 + [vmem] * 12,
        out_specs=vmem,
        scratch_shapes=[
            pltpu.SMEM((LOC,), jnp.int32),
            pltpu.VMEM((1, T), jnp.int32),
            pltpu.VMEM((8, S, T), F32),
            pltpu.VMEM((2, 24, T), F32),
        ] + [pltpu.VMEM((len(some) + 1, 1 if i else 2, T), F32) for i, some in enumerate(offsets)] + [
            pltpu.VMEM((1 if i else 2, T), F32) for i in range(len(offsets))] + [
            pltpu.SemaphoreType.DMA((2,)),
            pltpu.SemaphoreType.DMA((count,)),
            pltpu.SemaphoreType.DMA((count,)),
        ],
        compiler_params=pltpu.CompilerParams(vmem_limit_bytes=24 << 20, collective_id=1, has_side_effects=True),
        name="tail",
    )(*map(stay, (parents, weights.reshape(1, T))), handed, info, factor, msg, w_loc, m_loc, y_loc, eig_w, inv_w, basis, lam, freq)
    local, top, loglik = pl.pallas_call(
        finish,
        out_shape=(shape((1, LOC), F32), shape((1, TOP), F32), shape((1, T), F32)),
        in_specs=[vmem],
        out_specs=(vmem,) * 3,
        compiler_params=pltpu.CompilerParams(vmem_limit_bytes=4 << 20),
        name="finish",
    )(rows)
    return local.reshape(LOC), top.reshape(TOP), loglik.reshape(T)


def solution(mesh):
    placed = (P("leaf", None, "site"), P("leaf"), P("leaf"), P(), P(), P("site"), P(), P(), P(), P(), P())
    return jax.shard_map(
        on_device,
        mesh=mesh,
        in_specs=placed,
        out_specs=(P("leaf"), P(), P("site")),
        check_vma=False,
    )
```

```python
import functools

import jax
import jax.numpy as jnp
from jax import lax
from jax.experimental import pallas as pl
from jax.experimental.pallas import tpu as pltpu
from jax.sharding import PartitionSpec as P

CODONS = 61
S = 64
T = 128
LEAVES = 8
LOC = 14
GROUPS = 64
TOP = 126
ROOT = 126
WIN = 6
NARROW = 3
TURN = 102
ACROSS = 16
F32 = jnp.float32
BF16 = jnp.bfloat16
PRECISE = lax.Precision.HIGHEST
NX, NZ = 4, 8
MESH = pl.DeviceIdType.MESH


def split(u):
    high = u.astype(BF16)
    low = (u - high.astype(F32)).astype(BF16)
    return high, low


def apply(w, u):
    high, low = split(u)
    return jnp.dot(w, jnp.concatenate([high, low, high, low], axis=0), preferred_element_type=F32)


def pack(doubled):
    high, low = split(doubled)
    return jnp.concatenate([high, low], axis=1)


def double(a):
    return jnp.concatenate([a, a], axis=1)


def dot(a, b):
    return jnp.dot(a, b, precision=PRECISE, preferred_element_type=F32)


def growth(x):
    series = 1.0 + x * (1 / 2 + x * (1 / 6 + x * (1 / 24 + x * (1 / 120 + x * (
        1 / 720 + x * (1 / 5040 + x * (1 / 40320)))))))
    small = jnp.abs(x) < 0.5
    safe = jnp.where(small, 1.0, x)
    return jnp.where(small, series, (jnp.exp(x) - 1.0) / safe)


def iota(shape, axis):
    return lax.broadcasted_iota(jnp.int32, shape, axis)


def column(row):
    n = row.shape[1]
    eye = iota((n, n), 0) == iota((n, n), 1)
    return jnp.sum(jnp.where(eye, row, jnp.zeros_like(row)), axis=1, keepdims=True)


def biggest(u):
    used = iota((S, T), 0) < CODONS
    return jnp.max(jnp.where(used, u, 0.0), axis=0, keepdims=True)


def inverse(row):
    return pltpu.reciprocal(row, approx=True)


def held_integrals(basis2, lam2, lam_col, t):
    spread = (lam_col - lam2) * t
    return pack(basis2 * (t * jnp.exp(lam2 * t) * growth(spread)))


def local_children(parents, node):
    late, early = jnp.int32(0), jnp.int32(0)
    for c in range(LOC):
        hit = parents[c] == node
        early = jnp.where(hit, late, early)
        late = jnp.where(hit, c, late)
    return late, early


def slot_of(x, z, c):
    return c * (NX * NZ) + z * NX + x


def prepare(parents_h, lengths_h, top_lengths_h, top_parents_h, tips_h, vectors_h, inverse_h, lam_h, rates_h, freq_h,
            msg, w_top, w_loc, m_loc, y_loc, links, eig_w, inv_w, basis_out, lam_out, freq_out,
            parents, lengths, top_lengths, top_parents, tips, vectors, inverse_vectors, lam, rates, freq, x_int,
            in_sem, send_sem, recv_sem):
    me = lax.axis_index("leaf")
    site = lax.axis_index("site")
    core = lax.rem(me, 2)
    z = lax.rem(me // 2, NZ)
    x = me // (2 * NZ)

    loads = [pltpu.make_async_copy(src, dst, in_sem.at[i]) for i, (src, dst) in enumerate((
        (vectors_h, vectors), (inverse_h, inverse_vectors), (lam_h, lam), (lengths_h, lengths),
        (top_lengths_h, top_lengths), (tips_h, tips), (parents_h, parents), (rates_h, rates),
        (top_parents_h, top_parents), (freq_h, freq)))]
    for load in loads:
        load.start()

    def device(dx, dz, dc):
        nx, nz = lax.rem(x + dx + NX, NX), lax.rem(z + dz + NZ, NZ)
        nc = 1 - core if dc else core
        return ((nx * NZ + nz) * 2 + nc, site)

    x_peers = [(dx, 0, 0) for dx in (1, 2, 3)]
    partners = x_peers + [(0, dz, 0) for dz in range(1, NZ)] + [(0, 0, 1)]
    barrier = pltpu.get_barrier_semaphore()
    for partner in partners:
        pl.semaphore_signal(barrier, inc=1, device_id=device(*partner), device_id_type=MESH)

    for load in loads[:7]:
        load.wait()
    lam_row = lam[...]
    lam_col = column(lam_row)
    lam2 = double(lam_row)
    used = iota((S, S), 0) < CODONS
    right = jnp.where(used, vectors[...], 0.0)
    left = inverse_vectors[...]
    right2 = double(right)
    left_high, left_low = split(double(left))
    left_stack = jnp.concatenate([left_high, left_low, left_high, left_low], axis=0)
    r2, c2 = iota((S, T), 0), iota((S, T), 1)
    eye2 = jnp.where((r2 < CODONS) & ((r2 == c2) | (r2 + S == c2)), 1.0, 0.0)

    def branches(ts):
        scaled = []
        for t in ts:
            arg = lam2 * t
            scaled.append(pack(right2 * (arg * growth(arg))))
        result = jnp.dot(jnp.concatenate(scaled, axis=0), left_stack, preferred_element_type=F32)
        return [pack(eye2 + result[S * i:S * (i + 1)]) for i in range(len(ts))]

    for c, w in enumerate(branches([lengths[c] for c in range(LEAVES)])):
        w_loc[c] = w
        m_loc[c] = apply(w, tips[c])
    inner = branches([lengths[c] for c in range(LEAVES, LOC)] + [top_lengths[me]])
    for c, w in enumerate(inner):
        w_loc[LEAVES + c] = w
    factors = []
    for n in range(LEAVES, LOC + 1):
        a, b = local_children(parents, n)
        u = m_loc[a] * m_loc[b]
        r = inverse(biggest(u))
        factors.append(r)
        x_int[n - LEAVES] = u * r
        y = apply(w_loc[n], u) * r
        if n < LOC:
            m_loc[n] = y
        else:
            logs = -jnp.sum(jnp.log(jnp.concatenate(factors, axis=0)), axis=0, keepdims=True)
            msg[slot_of(x, z, core)] = jnp.where(iota((S, T), 0) == S - 1, logs, y)
    pl.semaphore_wait(barrier, len(partners))

    counter = [0]

    main, rest = pl.ds(0, S - ACROSS), pl.ds(S - ACROSS, ACROSS)

    def block(bx, bz, bc, rows):
        return msg.at[slot_of(bx, bz, bc), rows]

    def group(bz, bc, rows):
        return msg.at[pl.ds(slot_of(0, bz, bc), NX), rows]

    started = []

    def send(piece, where, arriving):
        k = counter[0]
        counter[0] += 1
        copy = pltpu.make_async_remote_copy(src_ref=piece, dst_ref=piece, send_sem=send_sem.at[k],
                                            recv_sem=recv_sem.at[k], device_id=device(*where), device_id_type=MESH)
        copy.start()
        started.append(copy)
        incoming = pltpu.make_async_remote_copy(src_ref=arriving, dst_ref=arriving, send_sem=send_sem.at[k],
                                                recv_sem=recv_sem.at[k], device_id=device(*where), device_id_type=MESH)
        return incoming

    def at_z(dz):
        return lax.rem(z + dz + NZ, NZ)

    def at_x(dx):
        return lax.rem(x + dx + NX, NX)

    def along_z(dz):
        return send(block(x, z, core, main), (0, dz, 0), block(x, at_z(-dz), core, main))

    def along_x(dz, rows):
        return [send(block(x, at_z(-dz), core, rows), (dx, 0, 0), block(at_x(-dx), at_z(-dz), core, rows))
                for dx in (1, 3, 2)]

    def group_z(dz):
        return send(group(z, core, rest), (0, dz, 0), group(at_z(-dz), core, rest))

    def across(dz, rows):
        return send(group(at_z(-dz), core, rows), (0, 0, 1), group(at_z(-dz), 1 - core, rows))

    def shared():
        loads[7].wait()
        loads[8].wait()
        loads[9].wait()
        parent_col = column(top_parents[...])
        child = iota((TOP, T), 0)
        hit = parent_col == iota((TOP, T), 1)
        late = jnp.max(jnp.where(hit, child, 0), axis=0, keepdims=True)
        early = jnp.min(jnp.where(hit, child, TOP), axis=0, keepdims=True)
        pair = jnp.concatenate([late, early, jnp.zeros((6, T), jnp.int32)], axis=0)
        slots = (pair & 1) * (NX * NZ) + ((pair >> 1) & (NZ - 1)) * NX + (pair >> 4)
        pair = jnp.where(pair < GROUPS, slots, pair)
        lane = iota((8, T), 1)
        links[...] = jnp.where((lane >= GROUPS) & (lane <= ROOT), pair, 0)
        freq_out[...] = jnp.broadcast_to(column(freq[...]), (S, T))
        lam_out[...] = jnp.broadcast_to(lam2, (8, T))
        basis_out[...] = double(dot(dot(left, rates[...]), right))
        eig_w[...] = pack(right2)
        inv_w[...] = pack(double(left))

    def products(lo, hi):
        for c in range(lo, hi):
            t = lengths[c] if c < LOC else top_lengths[me]
            v = apply(inv_w[...], tips[c] if c < LEAVES else x_int[c - LEAVES])
            y_loc[c] = apply(eig_w[...], apply(held_integrals(basis_out[...], lam2, lam_col, t), v))

    def matrices(lo, hi):
        def some(i, _):
            ts = [top_lengths[jnp.minimum(GROUPS + i * 8 + j, TOP - 1)] for j in range(8)]
            for j, w in enumerate(branches(ts)):
                w_top[i * 8 + j] = w
            return 0

        lax.fori_loop(lo, hi, some, 0)

    order = (1, -1, 2, -2, 3, -3, 4)
    turns = (0,) + order
    first = along_x(0, rest)
    from_z = {dz: along_z(dz) for dz in order[:2]}
    from_x = {0: along_x(0, main)}
    from_z.update({dz: along_z(dz) for dz in order[2:]})
    crossed = []
    closed = [0]

    def close():
        dz = turns[closed[0]]
        closed[0] += 1
        for one in from_x[dz]:
            one.wait_recv()
        crossed.append(across(dz, main))

    shared()
    for i, dz in enumerate(order):
        from_z[dz].wait_recv()
        from_x[dz] = along_x(dz, main)
        if i == 0:
            for one in first:
                one.wait_recv()
            groups = {d: group_z(d) for d in order}
            crossed.append(across(0, rest))
        if i >= 5:
            close()
        if i in (1, 3, 5):
            matrices(i - 1, i + 1)
    products(0, 5)
    for i, dz in enumerate(order):
        groups[dz].wait_recv()
        crossed.append(across(dz, rest))
        if closed[0] < len(turns):
            close()
        if i == 1:
            products(5, 10)
        if i == 3:
            products(10, 15)
        if i == 5:
            matrices(6, 8)
    while closed[0] < len(turns):
        close()
    for one in crossed:
        one.wait_recv()
    for one in started:
        one.wait_send()


COPIES = 3 * (NZ + 1) + 2 * (NZ - 1) + 2 * NZ


def joining(top_parents_h, top_lengths_h, links, msg_in, w_top, handed, info, factor, msg,
            top_parents, top_lengths, path, arrs, sem):
    del msg_in
    loads = [pltpu.make_async_copy(src, dst, sem.at[i]) for i, (src, dst) in enumerate((
        (top_parents_h, top_parents), (top_lengths_h, top_lengths)))]
    for load in loads:
        load.start()
    me = lax.axis_index("leaf")
    slot = slot_of(me // (2 * NZ), lax.rem(me // 2, NZ), lax.rem(me, 2))
    factor[...] = jnp.ones((72, T), F32)
    def late(n):
        return links[0, n]

    def early(n):
        return links[1, n]

    def climb(width, n):
        done = []
        fits = True
        steps = jnp.int32(1)
        for j in range(width):
            k = jnp.minimum(n + j, T - 1) if j > 1 else n + j
            a, b = late(k), early(k)
            if j:
                fits = fits & (a < n)
                steps = steps + fits.astype(jnp.int32)
            u = msg[a] * msg[b]
            y = apply(w_top[jnp.minimum(k, ROOT) - GROUPS], u)
            r = inverse(biggest(u))
            done.append((y * r, r))
        for j, (y, r) in enumerate(done):
            msg[n + j] = y
            factor[pl.ds(n + j - GROUPS, 1)] = r
        return n + steps

    reached = lax.while_loop(lambda n: n < TURN, functools.partial(climb, WIN), jnp.int32(GROUPS))
    lax.while_loop(lambda n: n < ROOT, functools.partial(climb, NARROW), reached)

    for load in loads:
        load.wait()

    def walk(state):
        c, depth, mine, at = state
        path[depth] = c
        p = top_parents[jnp.where(depth == 0, me, c)]
        found = (mine < 0) & (late(p) == c)
        return (p, depth + 1, jnp.where(found, p, mine), jnp.where(found, depth + 1, at))

    _, depth, mine, at = lax.while_loop(
        lambda state: state[0] != ROOT, walk, (slot, jnp.int32(0), jnp.int32(-1), jnp.int32(0)))
    counted = (mine >= 0) & (mine < ROOT)
    node = jnp.where(counted, mine, GROUPS)
    at = jnp.where(counted, at, 0)

    def step_down(i, o):
        k = depth - 1 - i
        c = path[k]
        p = top_parents[c]
        arriving = o * msg[late(p) + early(p) - c]
        arrs[k] = arriving
        return apply(w_top[c - GROUPS], arriving) * inverse(biggest(arriving))

    o = lax.fori_loop(0, depth - 1, step_down, jnp.ones((S, T), F32))
    p = top_parents[me]
    leaf_arriving = o * msg[late(p) + early(p) - slot]
    arrs[0] = leaf_arriving
    handed[0] = leaf_arriving
    handed[1] = msg[slot]
    handed[2] = arrs[at]
    handed[3] = msg[node]
    handed[4] = msg[late(node)] * msg[early(node)] * factor[pl.ds(node - GROUPS, 1)]
    handed[5] = msg[late(ROOT)] * msg[early(ROOT)]
    row = iota((8, T), 0)
    info[...] = jnp.where(row == 0, top_lengths[node], jnp.where(counted, node, -1).astype(F32))


PHASES = ("yc", "x", "z")


def tail(parents_h, weights_h, handed, info, factor, msg, w_loc, m_loc, y_loc, eig_w, inv_w, basis, lam, freq, out,
         parents, weights, o_loc, rows, *rest):
    bufs, parts = rest[:len(PHASES)], rest[len(PHASES):2 * len(PHASES)]
    in_sem, send_sem, recv_sem = rest[2 * len(PHASES):]
    loads = [pltpu.make_async_copy(parents_h, parents, in_sem.at[0]), pltpu.make_async_copy(weights_h, weights, in_sem.at[1])]
    for load in loads:
        load.start()
    me = lax.axis_index("leaf")
    sizes = {"x": NX, "z": NZ, "c": 2, "y": lax.axis_size("site")}
    here = {"x": me // (2 * NZ), "z": lax.rem(me // 2, NZ), "c": lax.rem(me, 2), "y": lax.axis_index("site")}

    def shifted(offset):
        return {a: (lax.rem(here[a] + offset.get(a, 0) + sizes[a], sizes[a])) for a in here}

    def device(offset):
        at = shifted(offset)
        return ((at["x"] * NZ + at["z"]) * 2 + at["c"], at["y"])

    def place(axes, at):
        index = 0
        for a in axes:
            index = index * sizes[a] + at[a]
        return index

    offsets = [phase_offsets(axes, sizes) for axes in PHASES]
    barrier = pltpu.get_barrier_semaphore()
    for some in offsets:
        for offset in some:
            pl.semaphore_signal(barrier, inc=1, device_id=device(offset), device_id_type=MESH)

    freq_col = freq[...]

    def ratio(row, arriving, message, y):
        weighted = freq_col * arriving
        rows[0, pl.ds(row, 1)] = jnp.sum(weighted * y, axis=0, keepdims=True)
        rows[1, pl.ds(row, 1)] = jnp.sum(weighted * message, axis=0, keepdims=True)

    rows[...] = jnp.ones((2, 24, T), F32)
    lam2 = lam[0:1]
    o_loc[LOC - LEAVES] = apply(w_loc[LOC], handed[0]) * inverse(biggest(handed[0]))
    ratio(16, handed[0], handed[1], y_loc[LOC])
    held = held_integrals(basis[...], lam2, column(lam2[:, :S]), info[0:1, 0:1])
    ratio(17, handed[2], handed[3], apply(eig_w[...], apply(held, apply(inv_w[...], handed[4]))))
    for load in loads:
        load.wait()
    for c in range(LOC - 1, -1, -1):
        p = jnp.clip(parents[c], LEAVES, LOC)
        sibling = jnp.int32(0)
        for other in range(LOC):
            if other != c:
                sibling = jnp.where(parents[other] == p, other, sibling)
        arriving = o_loc[p - LEAVES] * m_loc[sibling]
        if c >= LEAVES:
            o_loc[c - LEAVES] = apply(w_loc[c], arriving) * inverse(biggest(arriving))
        ratio(c, arriving, m_loc[c], y_loc[c])
    weight = weights[...].astype(F32)
    expected = jnp.where(iota((24, T), 0) == LOC, weight, weight * rows[0] / rows[1])
    expected = jnp.concatenate([expected, jnp.zeros((T - 24, T), F32)], axis=0)
    sums = lax.dot_general(jnp.ones((8, T), F32), expected, (((1,), (1,)), ((), ())),
                           precision=PRECISE, preferred_element_type=F32)
    lane = iota((1, T), 1)
    node = info[1:2]
    top_row = jnp.where(lane == me, sums[0:1, 16:17], 0.0) + jnp.where(lane.astype(F32) == node, sums[0:1, 17:18], 0.0)
    parts[0][...] = jnp.concatenate([sums[0:1], top_row], axis=0)

    logs = [msg[g, pl.ds(S - 1, 1)] for g in range(GROUPS)]
    while len(logs) > 1:
        logs = [a + b for a, b in zip(logs[::2], logs[1::2])]
    inner = -jnp.sum(jnp.log(jnp.where(iota((72, T), 0) < TOP - GROUPS, factor[...], 1.0)), axis=0, keepdims=True)
    likelihood = jnp.sum(freq_col * handed[5], axis=0, keepdims=True)
    loglik = (jnp.log(likelihood) + inner + logs[0]) * (1.0 / (GROUPS * LEAVES))
    pl.semaphore_wait(barrier, sum(map(len, offsets)))

    k = 0
    copies = []
    for i, (axes, some) in enumerate(zip(PHASES, offsets)):
        buf, part = bufs[i], parts[i]
        mine = place(axes, here)
        buf[mine] = part[...]
        arrivals = []
        for offset in some:
            copy = pltpu.make_async_remote_copy(src_ref=part, dst_ref=buf.at[mine], send_sem=send_sem.at[k],
                                                recv_sem=recv_sem.at[k], device_id=device(offset), device_id_type=MESH)
            copy.start()
            copies.append(copy)
            there = buf.at[place(axes, shifted({a: -n for a, n in offset.items()}))]
            arrivals.append(pltpu.make_async_remote_copy(
                src_ref=there, dst_ref=there, send_sem=send_sem.at[k], recv_sem=recv_sem.at[k],
                device_id=device(offset), device_id_type=MESH))
            k += 1
        for arrival in arrivals:
            arrival.wait_recv()
        if i == 0:
            local = buf[here["c"], 0:1]
            total = buf[0, 1:2] + buf[1, 1:2]
            for n in range(1, sizes["y"]):
                local = local + buf[2 * n + here["c"], 0:1]
                total = total + (buf[2 * n, 1:2] + buf[2 * n + 1, 1:2])
            weight_total = local[:, LOC:LOC + 1]
        else:
            total = buf[0]
            for n in range(1, len(some) + 1):
                total = total + buf[n]
        if i + 1 < len(PHASES):
            parts[i + 1][...] = total
    out[...] = jnp.concatenate([local / weight_total, total / weight_total, loglik], axis=0)
    for copy in copies:
        copy.wait_send()


def finish(rows, local, top, loglik):
    local[...] = rows[0:1, :LOC]
    top[...] = rows[1:2, :TOP]
    loglik[...] = rows[2:3]


def phase_offsets(axes, sizes):
    found = [{}]
    for a in axes:
        found = [{**one, a: n} for one in found for n in range(sizes[a])]
    return [one for one in found if any(one.values())]


def on_device(tips, parents, branch_lengths, top_parents, top_lengths, weights, eig_vectors,
              eig_inverse, eig_values, labeled_rates, root_freq):
    hbm = pl.BlockSpec(memory_space=pltpu.HBM)
    stay = functools.partial(pltpu.with_memory_space_constraint, memory_space=pltpu.HBM)
    smem = pl.BlockSpec(memory_space=pltpu.SMEM)
    vmem = pl.BlockSpec(memory_space=pltpu.VMEM)
    shape = jax.ShapeDtypeStruct
    msg, *made = pl.pallas_call(
        prepare,
        out_shape=(
            shape((ROOT + 1 + WIN, S, T), F32),
            shape((GROUPS, S, 256), BF16),
            shape((LOC + 1, S, 256), BF16),
            shape((LOC, S, T), F32),
            shape((LOC + 1, S, T), F32),
            shape((8, T), jnp.int32),
            shape((S, 256), BF16),
            shape((S, 256), BF16),
            shape((S, T), F32),
            shape((8, T), F32),
            shape((S, T), F32),
        ),
        in_specs=[hbm] * 10,
        out_specs=(vmem,) * 11,
        scratch_shapes=[
            pltpu.SMEM((LOC,), jnp.int32),
            pltpu.SMEM((LOC,), F32),
            pltpu.SMEM((TOP,), F32),
            pltpu.VMEM((1, TOP), jnp.int32),
            pltpu.VMEM((LEAVES, S, T), F32),
            pltpu.VMEM((S, S), F32),
            pltpu.VMEM((S, S), F32),
            pltpu.VMEM((1, S), F32),
            pltpu.VMEM((S, S), F32),
            pltpu.VMEM((1, S), F32),
            pltpu.VMEM((8, S, T), F32),
            pltpu.SemaphoreType.DMA((10,)),
            pltpu.SemaphoreType.DMA((COPIES,)),
            pltpu.SemaphoreType.DMA((COPIES,)),
        ],
        compiler_params=pltpu.CompilerParams(vmem_limit_bytes=40 << 20, collective_id=0, has_side_effects=True),
        name="prepare",
    )(*map(stay, (parents, branch_lengths, top_lengths, top_parents.reshape(1, TOP), tips, eig_vectors, eig_inverse,
                   eig_values.reshape(1, S), labeled_rates, root_freq.reshape(1, S))))
    w_top, w_loc, m_loc, y_loc, links, eig_w, inv_w, basis, lam, freq = made
    handed, info, factor, msg = pl.pallas_call(
        joining,
        out_shape=(shape((6, S, T), F32), shape((8, T), F32), shape((72, T), F32), shape(msg.shape, F32)),
        in_specs=[hbm] * 2 + [smem] + [vmem] * 2,
        out_specs=(vmem,) * 4,
        input_output_aliases={3: 3},
        scratch_shapes=[
            pltpu.SMEM((TOP,), jnp.int32),
            pltpu.SMEM((TOP,), F32),
            pltpu.SMEM((64,), jnp.int32),
            pltpu.VMEM((GROUPS, S, T), F32),
            pltpu.SemaphoreType.DMA((2,)),
        ],
        compiler_params=pltpu.CompilerParams(vmem_limit_bytes=24 << 20),
        name="joining",
    )(*map(stay, (top_parents, top_lengths)), links, msg, w_top)
    sizes = {"x": NX, "z": NZ, "c": 2, "y": lax.axis_size("site")}
    offsets = [phase_offsets(axes, sizes) for axes in PHASES]
    count = sum(map(len, offsets))
    rows = pl.pallas_call(
        tail,
        out_shape=shape((3, T), F32),
        in_specs=[hbm] * 2 + [vmem] * 12,
        out_specs=vmem,
        scratch_shapes=[
            pltpu.SMEM((LOC,), jnp.int32),
            pltpu.VMEM((1, T), jnp.int32),
            pltpu.VMEM((8, S, T), F32),
            pltpu.VMEM((2, 24, T), F32),
        ] + [pltpu.VMEM((len(some) + 1, 1 if i else 2, T), F32) for i, some in enumerate(offsets)] + [
            pltpu.VMEM((1 if i else 2, T), F32) for i in range(len(offsets))] + [
            pltpu.SemaphoreType.DMA((2,)),
            pltpu.SemaphoreType.DMA((count,)),
            pltpu.SemaphoreType.DMA((count,)),
        ],
        compiler_params=pltpu.CompilerParams(vmem_limit_bytes=24 << 20, collective_id=1, has_side_effects=True),
        name="tail",
    )(*map(stay, (parents, weights.reshape(1, T))), handed, info, factor, msg, w_loc, m_loc, y_loc, eig_w, inv_w, basis, lam, freq)
    local, top, loglik = pl.pallas_call(
        finish,
        out_shape=(shape((1, LOC), F32), shape((1, TOP), F32), shape((1, T), F32)),
        in_specs=[vmem],
        out_specs=(vmem,) * 3,
        compiler_params=pltpu.CompilerParams(vmem_limit_bytes=4 << 20),
        name="finish",
    )(rows)
    return local.reshape(LOC), top.reshape(TOP), loglik.reshape(T)


def solution(mesh):
    placed = (P("leaf", None, "site"), P("leaf"), P("leaf"), P(), P(), P("site"), P(), P(), P(), P(), P())
    return jax.shard_map(
        on_device,
        mesh=mesh,
        in_specs=placed,
        out_specs=(P("leaf"), P(), P("site")),
        check_vma=False,
    )
```
